32 devices in a mesh: dp: 16 (over z, y, core), mp: 2 (over x).
Axes of the slice: x: 2, y: 2, z: 4, core: 2. Of those that a mesh axis runs over, the one named last changes fastest.
Arguments:
- image_small: bfloat16 [128, 196, 768], P('dp', None, 'mp')
- image_large: bfloat16 [32, 576, 768], P('dp', None, 'mp')
- image_counts: int32 [16, 2], P('dp'), may hold values from 0 to 8, as said below
- norm_gain: float32 [3, 2, 768], P(None, None, 'mp'), may hold values from 0.5 to 2
- norm_shift: float32 [3, 2, 768], P(None, None, 'mp'), may hold values from -3 to 3
- mix_in_small: bfloat16 [3, 196, 384], replicated, may hold values from -0.4375 to 0.4375
- mix_bias_small: float32 [3, 384], replicated, may hold values from -3 to 3
- mix_out_small: bfloat16 [3, 384, 196], replicated, may hold values from -0.3125 to 0.3125
- mix_obias_small: float32 [3, 196], replicated, may hold values from -3 to 3
- mix_in_large: bfloat16 [3, 576, 384], replicated, may hold values from -0.25 to 0.25
- mix_bias_large: float32 [3, 384], replicated, may hold values from -3 to 3
- mix_out_large: bfloat16 [3, 384, 576], replicated, may hold values from -0.3125 to 0.3125
- mix_obias_large: float32 [3, 576], replicated, may hold values from -3 to 3
- chan_in: bfloat16 [3, 768, 3072], P(None, None, 'mp'), may hold values from -0.21875 to 0.21875
- chan_bias: float32 [3, 3072], P(None, 'mp'), may hold values from -3 to 3
- chan_out: bfloat16 [3, 3072, 768], P(None, 'mp'), may hold values from -0.109375 to 0.109375
- chan_obias: float32 [3, 768], P(None, 'mp'), may hold values from -3 to 3
- cot_small: bfloat16 [128, 196, 768], P('dp', None, 'mp'), may hold values from -6 to 6
- cot_large: bfloat16 [32, 576, 768], P('dp', None, 'mp'), may hold values from -6 to 6
Outputs:
- out_small: bfloat16 [128, 196, 768], P('dp', None, 'mp')
- out_large: bfloat16 [32, 576, 768], P('dp', None, 'mp')
- grad_small: float32 [128, 196, 768], P('dp', None, 'mp')
- grad_large: float32 [32, 576, 768], P('dp', None, 'mp')
- grad_norm_gain: float32 [3, 2, 768], P(None, None, 'mp')
- grad_norm_shift: float32 [3, 2, 768], P(None, None, 'mp')
- grad_mix_in_small: float32 [3, 196, 384], replicated
- grad_mix_bias_small: float32 [3, 384], replicated
- grad_mix_out_small: float32 [3, 384, 196], replicated
- grad_mix_obias_small: float32 [3, 196], replicated
- grad_mix_in_large: float32 [3, 576, 384], replicated
- grad_mix_bias_large: float32 [3, 384], replicated
- grad_mix_out_large: float32 [3, 384, 576], replicated
- grad_mix_obias_large: float32 [3, 576], replicated
- grad_chan_in: float32 [3, 768, 3072], P(None, None, 'mp')
- grad_chan_bias: float32 [3, 3072], P(None, 'mp')
- grad_chan_out: float32 [3, 3072, 768], P(None, 'mp')
- grad_chan_obias: float32 [3, 768], P(None, 'mp')
The draws below stay inside these ranges and needn't reach their ends.
Inputs may be any that keep to these rules, and one draw needn't show every extreme that they name: `image_counts`: column 0 counts the live 224 pixel images of an index of dp, from 1 to 8; column 1 the live 384 pixel images, from 0 to 2; live images fill the first slots of that index; each column reaches its most on some index in every draw.
All inputs are finite; a program needn't handle non-finite values.
Results may differ from the reference program's by a relative error of at most 0.02.
Values may be sent and summed in bfloat16 or wider, within the bound.
No kernel may reach another device: no remote copies, remote signals or barrier semaphores. Data moves between devices by JAX's collectives and lax.ppermute only.
A program may use at most 448 MiB of HBM per device.

```python
import math
import jax
import jax.numpy as jnp
from jax import lax

C = 768
FFC = 3072
TH = 384
S1 = 196
S2 = 576
SMALL_DEV = 8
LARGE_DEV = 2
L = 3
NSMALL = 128
NLARGE = 32
N_DP = 16


def shaped_field(key, base_field, row_lo, row_hi):
    key_rows, key_chan = jax.random.split(key)
    channel_ramp = jnp.exp(jnp.linspace(math.log(0.5), math.log(1.5), C))
    chan_scale = channel_ramp * jax.random.uniform(key_chan, (C,), minval=0.6, maxval=1.6)
    row_scale = jnp.exp(jax.random.uniform(key_rows, base_field.shape[:2] + (1,), minval=math.log(row_lo), maxval=math.log(row_hi)))
    return base_field * row_scale * chan_scale


def draw_image_small(key, part):
    key = jax.random.fold_in(key, 1)
    key_base, key_rest = jax.random.split(key)
    base_field = jax.random.normal(key_base, (NSMALL, S1, C))
    return shaped_field(key_rest, base_field, 0.6, 1.6).astype(jnp.bfloat16)


def draw_image_large(key, part):
    key = jax.random.fold_in(key, 2)
    key_base, key_rest = jax.random.split(key)
    base_field = jax.random.normal(key_base, (NLARGE, S2, C))
    return shaped_field(key_rest, base_field, 0.6, 1.6).astype(jnp.bfloat16)


def draw_image_counts(key, part):
    key = jax.random.fold_in(key, 3)
    key_small, key_large, key_pick_small, key_pick_large = jax.random.split(key, 4)
    small_counts = jax.random.randint(key_small, (N_DP,), 1, SMALL_DEV + 1)
    large_counts = jax.random.randint(key_large, (N_DP,), 0, LARGE_DEV + 1)
    pick_small = jax.random.randint(key_pick_small, (), 0, N_DP)
    pick_large = jax.random.randint(key_pick_large, (), 0, N_DP)
    positions = jnp.arange(N_DP, dtype=jnp.int32)
    small_counts = jnp.where(positions == pick_small, SMALL_DEV, small_counts)
    large_counts = jnp.where(positions == pick_large, LARGE_DEV, large_counts)
    return jnp.stack([small_counts, large_counts], axis=1).astype(jnp.int32)


def block_levels(key, dims, shards, smallest, top_value):
    level, own = 1.0, jax.random.fold_in(key, 6)
    for position, shards_of in shards:
        heights = jnp.exp(jax.random.uniform(jax.random.fold_in(own, position), (shards_of,), jnp.float32, smallest / len(shards), top_value / len(shards)))
        level = level * jnp.repeat(heights, dims[position] // shards_of).reshape([-1 if axis == position else 1 for axis in range(len(dims))])
    return level


def bell_draw(stream_key, extent, scale, limit, cuts=(), kind=jnp.bfloat16):
    result = jax.random.normal(stream_key, extent, jnp.float32) * scale
    if len(cuts) > 0:
        result = block_levels(stream_key, extent, cuts, -0.22, 0.18) * result
    return jnp.clip(result, min=-limit, max=limit).astype(kind)


def setup_inputs(seed: int = 0) -> dict:
    splits = jax.random.split(jax.random.key(seed), 20)
    return {
        "image_small": draw_image_small(jax.random.fold_in(splits[19], 71), 0),
        "image_large": draw_image_large(jax.random.fold_in(splits[19], 71), 0),
        "image_counts": draw_image_counts(jax.random.fold_in(splits[19], 71), 0),
        "norm_gain": jnp.clip(jnp.exp(math.log(2.0) - 1.3862944 * jax.random.uniform(splits[3], (L, 2, C), jnp.float32) ** block_levels(splits[3], (L, 2, C), ((2, 2),), -0.2, 0.2)), 0.5, 2.0),
        "norm_shift": bell_draw(splits[4], (L, 2, C), 0.5, 3.0, ((2, 2),), jnp.float32),
        "mix_in_small": bell_draw(splits[5], (L, S1, TH), S1 ** -0.5, 0.4375),
        "mix_bias_small": bell_draw(splits[6], (L, TH), 0.5, 3.0, (), jnp.float32),
        "mix_out_small": bell_draw(splits[7], (L, TH, S1), TH ** -0.5, 0.3125),
        "mix_obias_small": bell_draw(splits[8], (L, S1), 0.5, 3.0, (), jnp.float32),
        "mix_in_large": bell_draw(splits[9], (L, S2, TH), S2 ** -0.5, 0.25),
        "mix_bias_large": bell_draw(splits[10], (L, TH), 0.5, 3.0, (), jnp.float32),
        "mix_out_large": bell_draw(splits[11], (L, TH, S2), TH ** -0.5, 0.3125),
        "mix_obias_large": bell_draw(splits[12], (L, S2), 0.5, 3.0, (), jnp.float32),
        "chan_in": bell_draw(splits[13], (L, C, FFC), C ** -0.5, 0.21875, ((2, 2),)),
        "chan_bias": bell_draw(splits[14], (L, FFC), 0.5, 3.0, ((1, 2),), jnp.float32),
        "chan_out": bell_draw(splits[15], (L, FFC, C), FFC ** -0.5, 0.109375, ((1, 2),)),
        "chan_obias": bell_draw(splits[16], (L, C), 0.5, 3.0, ((1, 2),), jnp.float32),
        "cot_small": bell_draw(splits[17], (NSMALL, S1, C), 1.0, 6.0, ((0, 16), (2, 2))),
        "cot_large": bell_draw(splits[18], (NLARGE, S2, C), 1.0, 6.0, ((0, 16), (2, 2))),
    }


EPS = 1e-06
HIGH = lax.Precision.HIGHEST
F32 = jnp.float32

@jax.custom_vjp
def low(v):
    return lax.optimization_barrier(v.astype(jnp.bfloat16)).astype(jnp.float32)

@jax.custom_vjp
def low_back(v):
    return v

def low_keep(v):
    return (low(v), None)

def low_pass(kept, grad):
    return (grad,)

def back_keep(v):
    return (v, None)

def back_low(kept, grad):
    return (low(grad),)
low.defvjp(low_keep, low_pass)
low_back.defvjp(back_keep, back_low)

def layer_norm(field, scale_vec, shift_vec):
    row_mean = lax.optimization_barrier(jnp.mean(field, axis=-1, keepdims=True))
    row_var = lax.optimization_barrier(jnp.mean((field - row_mean) ** 2, axis=-1, keepdims=True))
    return (field - row_mean) * lax.rsqrt(row_var + EPS) * scale_vec + shift_vec

def gelu_exact(field):
    return jax.nn.gelu(field, approximate=False)

def mixer_layer(field, layer_pos, params, set_index):
    gain_all, shift_all, mixers, chan_w_in, chan_b_in, chan_w_out, chan_b_out = params
    token_in, token_bias, token_out, token_obias = mixers[set_index]
    normed = low(layer_norm(field, gain_all[layer_pos, 0], shift_all[layer_pos, 0]))
    pre_act = low_back(jnp.einsum('nsc,sh->nhc', normed, token_in[layer_pos], precision=HIGH) + token_bias[layer_pos][None, :, None])
    activated = low(gelu_exact(pre_act))
    branch = low_back(jnp.einsum('nhc,hs->nsc', activated, token_out[layer_pos], precision=HIGH) + token_obias[layer_pos][None, :, None])
    mixed_rows = field + branch
    normed_rows = low(layer_norm(mixed_rows, gain_all[layer_pos, 1], shift_all[layer_pos, 1]))
    hidden = low_back(jnp.einsum('nsc,cf->nsf', normed_rows, chan_w_in[layer_pos], precision=HIGH) + chan_b_in[layer_pos])
    hidden_low = low(gelu_exact(hidden))
    channel_out = low_back(jnp.einsum('nsf,fc->nsc', hidden_low, chan_w_out[layer_pos], precision=HIGH) + chan_b_out[layer_pos])
    return mixed_rows + channel_out

def block_forward(small_in, large_in, params, live_small, live_large):
    for layer_pos in range(L):
        small_in = mixer_layer(small_in, layer_pos, params, 0)
        large_in = mixer_layer(large_in, layer_pos, params, 1)
    return (small_in * live_small, large_in * live_large)

def reference(image_small, image_large, image_counts, norm_gain, norm_shift, mix_in_small, mix_bias_small, mix_out_small, mix_obias_small, mix_in_large, mix_bias_large, mix_out_large, mix_obias_large, chan_in, chan_bias, chan_out, chan_obias, cot_small, cot_large):
    params = jax.tree.map(lambda array: array.astype(F32), (norm_gain, norm_shift, ((mix_in_small, mix_bias_small, mix_out_small, mix_obias_small), (mix_in_large, mix_bias_large, mix_out_large, mix_obias_large)), chan_in, chan_bias, chan_out, chan_obias))
    small_groups = image_small.astype(F32).reshape(N_DP, SMALL_DEV, S1, C)
    large_groups = image_large.astype(F32).reshape(N_DP, LARGE_DEV, S2, C)
    cot_small_groups = cot_small.astype(F32).reshape(N_DP, SMALL_DEV, S1, C)
    cot_large_groups = cot_large.astype(F32).reshape(N_DP, LARGE_DEV, S2, C)

    def group_step(totals, group_item):
        small_now, large_now, cot_small_now, cot_large_now, counts = group_item
        live_small = (jnp.arange(SMALL_DEV, dtype=jnp.int32) < counts[0]).astype(F32)[:, None, None]
        live_large = (jnp.arange(LARGE_DEV, dtype=jnp.int32) < counts[1]).astype(F32)[:, None, None]

        def forward(small_in, large_in, weights):
            return block_forward(small_in, large_in, weights, live_small, live_large)
        outputs, pullback = jax.vjp(forward, small_now, large_now, params)
        grad_small_now, grad_large_now, grad_params = pullback((cot_small_now, cot_large_now))
        return (jax.tree.map(jnp.add, totals, grad_params), (outputs[0], outputs[1], grad_small_now, grad_large_now))
    totals, stacked = lax.scan(group_step, jax.tree.map(jnp.zeros_like, params), (small_groups, large_groups, cot_small_groups, cot_large_groups, image_counts))
    outs_small, outs_large, grads_small, grads_large = stacked
    gain_grad, shift_grad, mix_sets, chan_in_grad, chan_bias_grad, chan_out_grad, chan_obias_grad = totals
    return (outs_small.reshape(NSMALL, S1, C).astype(jnp.bfloat16), outs_large.reshape(NLARGE, S2, C).astype(jnp.bfloat16), grads_small.reshape(NSMALL, S1, C), grads_large.reshape(NLARGE, S2, C), gain_grad, shift_grad, mix_sets[0][0], mix_sets[0][1], mix_sets[0][2], mix_sets[0][3], mix_sets[1][0], mix_sets[1][1], mix_sets[1][2], mix_sets[1][3], chan_in_grad, chan_bias_grad, chan_out_grad, chan_obias_grad)
```

```python
import functools

import jax
import jax.numpy as jnp
from jax import lax
from jax.experimental import pallas as pl
from jax.experimental.pallas import tpu as pltpu
from jax.sharding import PartitionSpec as P

EPS = 1e-06
F32 = jnp.float32
B16 = jnp.bfloat16


def gelu_exact(field):
    return jax.nn.gelu(field, approximate=False)


def gelu_pull(point, grad_in):
    return jax.vjp(gelu_exact, point)[1](grad_in)[0]


def norm_apply(stream, gain_vec, shift_vec, feature_count):
    totals = lax.psum(
        (
            jnp.sum(stream[0], -1),
            jnp.sum(stream[0] * stream[0], -1),
            jnp.sum(stream[1], -1),
            jnp.sum(stream[1] * stream[1], -1),
        ),
        "mp",
    )
    centred_list, scale_list, normed_list = ([], [], [])
    for set_index in range(2):
        row_mean = totals[2 * set_index] / feature_count
        spread = totals[2 * set_index + 1] / feature_count - row_mean * row_mean
        row_scale = lax.rsqrt(spread + EPS)
        centred = (stream[set_index] - row_mean[..., None]) * row_scale[..., None]
        centred_list.append(centred)
        scale_list.append(row_scale)
        normed_list.append(centred * gain_vec + shift_vec)
    return (centred_list, scale_list, normed_list)


def norm_back(grad_list, centred_list, scale_list, gain_vec, feature_count):
    scaled = [grad_list[0] * gain_vec, grad_list[1] * gain_vec]
    totals = lax.psum(
        (
            jnp.sum(scaled[0], -1),
            jnp.sum(scaled[0] * centred_list[0], -1),
            jnp.sum(scaled[1], -1),
            jnp.sum(scaled[1] * centred_list[1], -1),
        ),
        "mp",
    )
    back_list = []
    for set_index in range(2):
        inner_term = (
            scaled[set_index]
            - totals[2 * set_index][..., None] / feature_count
            - centred_list[set_index] * (totals[2 * set_index + 1][..., None] / feature_count)
        )
        back_list.append(scale_list[set_index][..., None] * inner_term)
    gain_grad = jnp.sum(grad_list[0] * centred_list[0], axis=(0, 1)) + jnp.sum(
        grad_list[1] * centred_list[1], axis=(0, 1)
    )
    shift_grad = jnp.sum(grad_list[0], axis=(0, 1)) + jnp.sum(grad_list[1], axis=(0, 1))
    return (back_list, gain_grad, shift_grad)


def split_body(
    image_small,
    image_large,
    image_counts,
    norm_gain,
    norm_shift,
    mix_in_small,
    mix_bias_small,
    mix_out_small,
    mix_obias_small,
    mix_in_large,
    mix_bias_large,
    mix_out_large,
    mix_obias_large,
    chan_in,
    chan_bias,
    chan_out,
    chan_obias,
    cot_small,
    cot_large,
):
    feature_count = norm_gain.shape[2] * lax.axis_size("mp")
    layers = norm_gain.shape[0]
    slot_count = (image_small.shape[0], image_large.shape[0])
    live_masks = [
        (jnp.arange(slot_count[k], dtype=jnp.int32) < image_counts[0, k]).astype(F32)[:, None, None]
        for k in range(2)
    ]
    mixers = (
        (mix_in_small, mix_bias_small, mix_out_small, mix_obias_small),
        (mix_in_large, mix_bias_large, mix_out_large, mix_obias_large),
    )
    stream = [image_small.astype(F32), image_large.astype(F32)]
    kept_state = []
    for layer_pos in range(layers):
        centred_one, scale_one, normed_one = norm_apply(
            stream, norm_gain[layer_pos, 0], norm_shift[layer_pos, 0], feature_count
        )
        lowered, pre_list, act_list, mixed_list = ([], [], [], [])
        for set_index in range(2):
            token_in, token_bias, token_out, token_obias = mixers[set_index]
            normed_low = normed_one[set_index].astype(B16)
            pre_act = (
                jnp.einsum(
                    "nsc,sh->nhc", normed_low, token_in[layer_pos], preferred_element_type=F32
                )
                + token_bias[layer_pos][None, :, None]
            )
            activated = gelu_exact(pre_act).astype(B16)
            branch = jnp.einsum(
                "nhc,hs->nsc", activated, token_out[layer_pos], preferred_element_type=F32
            )
            mixed_list.append(stream[set_index] + branch + token_obias[layer_pos][None, :, None])
            lowered.append(normed_low)
            pre_list.append(pre_act)
            act_list.append(activated)
        centred_two, scale_two, normed_two = norm_apply(
            mixed_list, norm_gain[layer_pos, 1], norm_shift[layer_pos, 1], feature_count
        )
        normed_rows = (normed_two[0].astype(B16), normed_two[1].astype(B16))
        weight_in = chan_in[layer_pos]
        gathered_rows = None
        hidden = (
            jnp.dot(
                lax.all_gather(normed_rows[0], "mp", axis=2, tiled=True),
                weight_in,
                preferred_element_type=F32,
            ),
            jnp.dot(
                lax.all_gather(normed_rows[1], "mp", axis=2, tiled=True),
                weight_in,
                preferred_element_type=F32,
            ),
        )
        hidden = [hidden[k] + chan_bias[layer_pos] for k in range(2)]
        hidden_low = [gelu_exact(hidden[k]).astype(B16) for k in range(2)]
        partial_value = [
            jnp.dot(hidden_low[k], chan_out[layer_pos], preferred_element_type=F32)
            for k in range(2)
        ]
        summed = (
            lax.psum_scatter(
                partial_value[0].astype(jnp.bfloat16), "mp", scatter_dimension=2, tiled=True
            ).astype(jnp.float32),
            lax.psum_scatter(
                partial_value[1].astype(jnp.bfloat16), "mp", scatter_dimension=2, tiled=True
            ).astype(jnp.float32),
        )
        kept_state.append(
            (
                centred_one,
                scale_one,
                lowered,
                pre_list,
                act_list,
                centred_two,
                scale_two,
                normed_rows,
                gathered_rows,
                hidden,
                hidden_low,
            )
        )
        stream = [mixed_list[k] + summed[k] + chan_obias[layer_pos] for k in range(2)]
    out_list = [(stream[k] * live_masks[k]).astype(B16) for k in range(2)]
    grad_stream = [cot_small.astype(F32) * live_masks[0], cot_large.astype(F32) * live_masks[1]]
    mix_terms = [None] * layers
    chan_terms = [None] * layers
    for layer_pos in reversed(range(layers)):
        (
            centred_one,
            scale_one,
            lowered,
            pre_list,
            act_list,
            centred_two,
            scale_two,
            normed_rows,
            gathered_rows,
            hidden,
            hidden_low,
        ) = kept_state[layer_pos]
        grad_low = (grad_stream[0].astype(B16), grad_stream[1].astype(B16))
        obias_grad = jnp.sum(grad_low[0].astype(F32), axis=(0, 1)) + jnp.sum(
            grad_low[1].astype(F32), axis=(0, 1)
        )
        gathered_grad = (
            lax.all_gather(grad_low[0], "mp", axis=2, tiled=True),
            lax.all_gather(grad_low[1], "mp", axis=2, tiled=True),
        )
        out_grad = jnp.einsum(
            "nsf,nsc->fc", hidden_low[0], gathered_grad[0], preferred_element_type=F32
        ) + jnp.einsum("nsf,nsc->fc", hidden_low[1], gathered_grad[1], preferred_element_type=F32)
        hidden_grad = [
            gelu_pull(
                hidden[k],
                jnp.einsum(
                    "nsc,fc->nsf", gathered_grad[k], chan_out[layer_pos], preferred_element_type=F32
                ),
            ).astype(B16)
            for k in range(2)
        ]
        bias_grad = jnp.sum(hidden_grad[0].astype(F32), axis=(0, 1)) + jnp.sum(
            hidden_grad[1].astype(F32), axis=(0, 1)
        )
        contribution = jnp.einsum(
            "nsk,nsf->kf",
            lax.all_gather(normed_rows[0], "mp", axis=2, tiled=True),
            hidden_grad[0],
            preferred_element_type=F32,
        ) + jnp.einsum(
            "nsk,nsf->kf",
            lax.all_gather(normed_rows[1], "mp", axis=2, tiled=True),
            hidden_grad[1],
            preferred_element_type=F32,
        )
        back_terms = [
            jnp.einsum(
                "nsf,cf->nsc", hidden_grad[k], chan_in[layer_pos], preferred_element_type=F32
            )
            for k in range(2)
        ]
        back_rows = (
            lax.psum_scatter(
                back_terms[0].astype(jnp.bfloat16), "mp", scatter_dimension=2, tiled=True
            ).astype(jnp.float32),
            lax.psum_scatter(
                back_terms[1].astype(jnp.bfloat16), "mp", scatter_dimension=2, tiled=True
            ).astype(jnp.float32),
        )
        norm_grad_two, gain_two, shift_two = norm_back(
            back_rows, centred_two, scale_two, norm_gain[layer_pos, 1], feature_count
        )
        mid_grad = [grad_stream[k] + norm_grad_two[k] for k in range(2)]
        token_terms = []
        norm_input = []
        for set_index in range(2):
            token_in, token_bias, token_out, token_obias = mixers[set_index]
            token_grad = mid_grad[set_index].astype(B16)
            token_obias_grad = jnp.sum(token_grad.astype(F32), axis=(0, 2))
            token_out_grad = jnp.einsum(
                "nhc,nsc->hs", act_list[set_index], token_grad, preferred_element_type=F32
            )
            act_grad = jnp.einsum(
                "nsc,hs->nhc", token_grad, token_out[layer_pos], preferred_element_type=F32
            )
            pre_grad = gelu_pull(pre_list[set_index], act_grad).astype(B16)
            token_bias_grad = jnp.sum(pre_grad.astype(F32), axis=(0, 2))
            token_in_grad = jnp.einsum(
                "nsc,nhc->sh", lowered[set_index], pre_grad, preferred_element_type=F32
            )
            norm_input.append(
                jnp.einsum("nhc,sh->nsc", pre_grad, token_in[layer_pos], preferred_element_type=F32)
            )
            token_terms += [token_in_grad, token_bias_grad, token_out_grad, token_obias_grad]
        norm_grad_one, gain_one, shift_one = norm_back(
            norm_input, centred_one, scale_one, norm_gain[layer_pos, 0], feature_count
        )
        grad_stream = [mid_grad[k] + norm_grad_one[k] for k in range(2)]
        chan_local = (
            contribution,
            bias_grad,
            out_grad,
            obias_grad,
            jnp.stack([gain_one, gain_two]),
            jnp.stack([shift_one, shift_two]),
        )
        mix_terms[layer_pos] = lax.psum(
            (
                token_terms[0],
                token_terms[1],
                token_terms[2],
                token_terms[3],
                token_terms[4],
                token_terms[5],
                token_terms[6],
                token_terms[7],
            ),
            ("dp", "mp"),
        )
        chan_terms[layer_pos] = (
            lax.psum(chan_local[0].astype(jnp.bfloat16), "dp").astype(jnp.float32),
            lax.psum(chan_local[1].astype(jnp.bfloat16), "dp").astype(jnp.float32),
            lax.psum(chan_local[2].astype(jnp.bfloat16), "dp").astype(jnp.float32),
            lax.psum(chan_local[3].astype(jnp.bfloat16), "dp").astype(jnp.float32),
            lax.psum(chan_local[4].astype(jnp.bfloat16), "dp").astype(jnp.float32),
            lax.psum(chan_local[5].astype(jnp.bfloat16), "dp").astype(jnp.float32),
        )
    mix_stacked = [jnp.stack([mix_terms[pos][item] for pos in range(layers)]) for item in range(8)]
    chan_stacked = [
        jnp.stack([chan_terms[pos][item] for pos in range(layers)]) for item in range(6)
    ]
    return (
        out_list[0],
        out_list[1],
        grad_stream[0],
        grad_stream[1],
        chan_stacked[4],
        chan_stacked[5],
        mix_stacked[0],
        mix_stacked[1],
        mix_stacked[2],
        mix_stacked[3],
        mix_stacked[4],
        mix_stacked[5],
        mix_stacked[6],
        mix_stacked[7],
        chan_stacked[0],
        chan_stacked[1],
        chan_stacked[2],
        chan_stacked[3],
    )


LANES = 128
SIDE, CORE, QUARTER, PLACE = range(4)
VMEM_LIMIT = 56 << 20
COST_SCALE = 200


def gelu_pair(point):
    below = 0.5 + 0.5 * lax.erf(point * 0.7071067811865476)
    bell = jnp.exp(point * point * -0.5) * 0.3989422804014327
    return point * below, below + point * bell


def kernel_call(
    kernel, grid, in_specs, out_specs, out_shape, scratch=(), cost=None, aliases=None, prefetch=0
):
    return pl.pallas_call(
        kernel,
        grid_spec=pltpu.PrefetchScalarGridSpec(
            num_scalar_prefetch=prefetch,
            grid=grid,
            in_specs=in_specs,
            out_specs=out_specs,
            scratch_shapes=list(scratch),
        ),
        out_shape=out_shape,
        compiler_params=pltpu.CompilerParams(vmem_limit_bytes=VMEM_LIMIT),
        cost_estimate=cost,
        input_output_aliases=aliases or {},
    )


def cost_of(flops, nbytes):
    return pl.CostEstimate(
        flops=int(COST_SCALE * flops), bytes_accessed=int(COST_SCALE * nbytes), transcendentals=0
    )


def mark_spec():
    return pl.BlockSpec(memory_space=pltpu.SMEM), jax.ShapeDtypeStruct((1, 1), F32)


def column(row, size):
    pad = -row.shape[1] % LANES
    if pad:
        row = jnp.concatenate([row, jnp.zeros((1, pad), F32)], 1)
    return jnp.broadcast_to(row, (8, row.shape[1])).T[:size, 0:1]


def pad_rows(value, size):
    if value.shape[0] == size:
        return value
    return jnp.concatenate([value, jnp.zeros((size - value.shape[0], value.shape[1]), value.dtype)], 0)


def dims_nt(left, right):
    return lax.dot_general(left, right, (((1,), (1,)), ((), ())), preferred_element_type=F32)


def dims_tn(left, right):
    return lax.dot_general(left, right, (((0,), (0,)), ((), ())), preferred_element_type=F32)


def dims_nn(left, right):
    return jnp.dot(left, right, preferred_element_type=F32)


def norm_block(field):
    centred = field - jnp.mean(field, -1, keepdims=True)
    scale = lax.rsqrt(jnp.mean(centred * centred, -1, keepdims=True) + EPS)
    return centred * scale, scale


def token_forward_kernel(x_ref, norm_ref, in_ref, bias_ref, out_ref, obias_ref, *rest):
    (
        mixed_ref,
        rows_ref,
        low_ref,
        act_ref,
        slope_ref,
        vhat_one_ref,
        vhat_two_ref,
        scale_ref,
        mark_ref,
    ) = rest[-9:]
    x = x_ref[...]
    size = x.shape[0]
    vhat, scale = norm_block(x)
    vhat_one_ref[...] = vhat.astype(B16)
    low = (vhat * norm_ref[0:1, :] + norm_ref[2:3, :]).astype(B16)
    low_ref[...] = low
    point = dims_tn(pad_rows(in_ref[...], size), low) + column(bias_ref[...], act_ref.shape[0])
    act, slope = gelu_pair(point)
    act = act.astype(B16)
    act_ref[...] = act
    slope_ref[...] = slope.astype(B16)
    mixed = x + dims_nn(pad_rows(out_ref[...], size), act) + column(obias_ref[...], size)
    mixed_ref[...] = mixed
    vhat, scale_two = norm_block(mixed)
    vhat_two_ref[...] = vhat.astype(B16)
    rows_ref[...] = (vhat * norm_ref[1:2, :] + norm_ref[3:4, :]).astype(B16)
    scale_ref[:, 0:1] = scale
    scale_ref[:, 1:2] = scale_two
    mark_ref[0, 0] = 0.0


def row_block(patches, width, offset):
    return pl.BlockSpec(
        (pl.Element(patches), pl.Element(width)),
        lambda i: ((offset // 16 + i * (patches // 16)) * 16, 0),
    )


def whole_spec(array):
    return pl.BlockSpec(array.shape, lambda *i: (0, 0))


def free_specs(arrays):
    return [pl.BlockSpec(memory_space=pl.ANY)] * len(arrays)


def layer_spec(array, pos):
    return pl.BlockSpec(
        (None,) + array.shape[1:], lambda *i: (pos,) + (0,) * (array.ndim - 1)
    )


def token_forward(x, pos, params, images, patches, offset, base, after=()):
    total, width = x.shape
    hidden = params[1].shape[2]
    rows = images * patches
    block = lambda size, lanes: pl.BlockSpec((size, lanes), lambda i: (i, 0))
    placed = row_block(patches, width, offset)
    shape = jax.ShapeDtypeStruct
    mark = mark_spec()
    return kernel_call(
        token_forward_kernel,
        (images,),
        [placed] + [layer_spec(a, pos) for a in params] + free_specs(base + after),
        [placed, placed]
        + [block(patches, width)]
        + [block(hidden, width)] * 2
        + [block(patches, width)] * 2
        + [block(patches, LANES), mark[0]],
        [
            shape((total, width), F32),
            shape((total, width), B16),
            shape((rows, width), B16),
            shape((images * hidden, width), B16),
            shape((images * hidden, width), B16),
            shape((rows, width), B16),
            shape((rows, width), B16),
            shape((rows, LANES), F32),
            mark[1],
        ],
        aliases={6 + i: i for i in range(len(base))},
        cost=cost_of(4 * rows * hidden * width, 30 * rows * width),
    )(x, *params, *base, *after)


def join_kernel(info_ref, own_ref, got_ref, live_ref, joined_ref, mark_ref):
    own, got = own_ref[...].astype(F32), got_ref[...].astype(F32)
    first = info_ref[SIDE] == 0
    live = live_ref[:, 0:1]
    half = own.shape[1]
    joined_ref[:, :half] = jnp.where(first, own, got) * live
    joined_ref[:, half:] = jnp.where(first, got, own) * live
    mark_ref[0, 0] = 0.0


def join_features(info, own, got, live, tiles=4):
    rows, half = own.shape
    block = lambda lanes: pl.BlockSpec((rows // tiles, lanes), lambda i, _: (i, 0))
    mark = mark_spec()
    return kernel_call(
        join_kernel,
        (tiles,),
        [block(half), block(half), block(LANES)],
        [block(2 * half), mark[0]],
        [jax.ShapeDtypeStruct((rows, 2 * half), F32), mark[1]],
        prefetch=1,
        cost=cost_of(0, 12 * rows * half),
    )(info, own, got, live)


def chan_forward_kernel(
    part,
    info_ref,
    rows_ref,
    mixed_ref,
    in_own_ref,
    out_own_ref,
    in_near_ref,
    in_far_ref,
    out_near_ref,
    out_far_ref,
    bias_ref,
    obias_ref,
    *rest,
):
    quant_ref, slope_ref, total_ref, in_other_ref, out_other_ref, mark_ref = rest[-6:]
    mark_ref[0, 0] = 0.0

    @pl.when(pl.program_id(0) == 0)
    def _():
        place = info_ref[QUARTER]
        for pieces, other_ref in (
            ((in_near_ref, in_far_ref), in_other_ref),
            ((out_near_ref, out_far_ref), out_other_ref),
        ):
            size = pieces[0].shape[1]
            for k in range(4):
                at = pl.multiple_of((place ^ k) * size, size)
                other_ref[pl.ds(at, size), :] = pieces[k // 2][k % 2]

    rows = rows_ref[...]
    total = mixed_ref[...] + obias_ref[...]
    units = in_own_ref.shape[1]
    for side, (in_ref, out_ref) in enumerate(
        ((in_own_ref, out_own_ref), (in_other_ref, out_other_ref))
    ):
        for at in range(0, units, part):
            lanes = slice(at, at + part)
            place = slice(side * units + at, side * units + at + part)
            point = dims_nn(rows, in_ref[:, lanes]) + bias_ref[:, place]
            quant, slope = gelu_pair(point)
            quant = quant.astype(B16)
            quant_ref[:, place] = quant
            slope_ref[:, place] = slope.astype(B16)
            total = total + dims_nn(quant, out_ref[lanes, :])
    total_ref[...] = total


def chan_forward(info, rows, mixed, own, found, layer, bias, obias, tile, part, after=()):
    pos, at = layer
    count, width = rows.shape
    units = bias.shape[2]
    half = units // 2
    mark = mark_spec()
    tiled = pl.BlockSpec((tile, width), lambda i, _: (i, 0))
    lanes = pl.BlockSpec((tile, units), lambda i, _: (i, 0))
    once = lambda rows, cols: pl.BlockSpec((rows, cols), lambda i, _: (0, 0))
    layered = lambda a: pl.BlockSpec((None,) + a.shape[1:], lambda i, _: (pos, 0, 0))
    pieces = lambda a: pl.BlockSpec(
        (a.shape[0], None) + a.shape[2:], lambda i, _: (0, at, 0, 0)
    )
    return kernel_call(
        functools.partial(chan_forward_kernel, part),
        (count // tile,),
        [tiled, tiled]
        + [layered(a) for a in own]
        + [pieces(a) for a in found]
        + [layered(bias), layered(obias)]
        + free_specs(after),
        [lanes, lanes, tiled, once(width, half), once(half, width), mark[0]],
        [
            jax.ShapeDtypeStruct((count, units), B16),
            jax.ShapeDtypeStruct((count, units), B16),
            jax.ShapeDtypeStruct((count, width), F32),
            jax.ShapeDtypeStruct((width, half), B16),
            jax.ShapeDtypeStruct((half, width), B16),
            mark[1],
        ],
        prefetch=1,
        cost=cost_of(4 * count * units * width, 4 * count * units + 10 * count * width),
    )(info, rows, mixed, *own, *found, bias, obias, *after)


def chan_backward_kernel(
    blocks,
    first,
    info_ref,
    grad_ref,
    rows_ref,
    quant_ref,
    slope_ref,
    in_own_ref,
    out_own_ref,
    in_other_ref,
    out_other_ref,
    *rest,
):
    sum_ref, small_ref, back_ref, mark_ref, low_ref = rest[-5:]
    mark_ref[0, 0] = 0.0
    step = pl.program_id(0)

    @pl.when(step == 0)
    def _():
        low = grad_ref[...].astype(B16)
        low_ref[...] = low
        small_ref[...] = jnp.zeros_like(small_ref)
        if first:
            small_ref[0:1, :] = jnp.sum(low.astype(F32), 0, keepdims=True)
            back_ref[...] = jnp.zeros_like(back_ref)
        else:
            back_ref[...] = rest[0][...]

    def body(other, in_ref, out_ref):
        low = low_ref[...]
        hidden = (dims_nt(low, out_ref[...]) * slope_ref[...].astype(F32)).astype(B16)
        core = 1 - info_ref[CORE] if first else info_ref[CORE]
        row = 1 + 2 * (info_ref[SIDE] ^ other) + core
        small_ref[pl.ds(row, 1), :] = jnp.sum(hidden.astype(F32), 0, keepdims=True)
        for item, grads in enumerate(
            (dims_tn(hidden, rows_ref[...]), dims_tn(quant_ref[...], low))
        ):
            place = info_ref[PLACE]
            size = grads.shape[0] // blocks
            for k in range(blocks):
                part = grads[k * size : (k + 1) * size, :].astype(B16)
                sum_ref[item, k ^ place] = part
        back_ref[...] += dims_nt(hidden, in_ref[...])

    pl.when(step == 0)(lambda: body(1, in_other_ref, out_other_ref))
    pl.when(step == 1)(lambda: body(0, in_own_ref, out_own_ref))


def chan_backward(
    info, grad, rows, quant, slope, own, other, pos, back, blocks, after=()
):
    count, width = rows.shape
    chunk = own[0].shape[2] // 2
    first = back is None
    core = lambda info: 1 - info[CORE] if first else info[CORE]
    lanes = pl.BlockSpec((count, chunk), lambda s, info: (0, 2 * (1 - s) + core(info)))
    once = lambda rows, cols: pl.BlockSpec((rows, cols), lambda s, _: (0, 0))
    part = (None, 2, blocks, chunk // blocks, width)
    sums = pl.BlockSpec(part, lambda s, _: (s,) + (0,) * (len(part) - 1))
    extra = () if first else (back,)
    mark = mark_spec()
    return kernel_call(
        functools.partial(chan_backward_kernel, blocks, first),
        (2,),
        [once(count, width), once(count, width), lanes, lanes]
        + [
            pl.BlockSpec((None, width, chunk), lambda s, info: (pos, 0, core(info))),
            pl.BlockSpec((None, chunk, width), lambda s, info: (pos, core(info), 0)),
            pl.BlockSpec((width, chunk), lambda s, info: (0, core(info))),
            pl.BlockSpec((chunk, width), lambda s, info: (core(info), 0)),
        ]
        + [once(count, width)] * len(extra)
        + free_specs(after),
        [sums, once(8, width), once(count, width), mark[0]],
        [
            jax.ShapeDtypeStruct((2,) + part[1:], B16),
            jax.ShapeDtypeStruct((8, width), F32),
            jax.ShapeDtypeStruct((count, width), F32),
            mark[1],
        ],
        scratch=[pltpu.VMEM((count, width), B16)],
        prefetch=1,
        cost=cost_of(16 * count * chunk * width, 8 * count * chunk + 16 * count * width),
    )(info, grad, rows, quant, slope, *own, *other, *extra, *after)


def assemble_kernel(places, size, all_ref, *rest):
    in_ref, out_ref, mark_ref, scratch = rest[-4:]
    mark_ref[0, 0] = 0.0

    def body(core):
        for i, (in_place, out_place) in enumerate(places):
            if i % 2 == core:
                at = slice(in_place * size, (in_place + 1) * size)
                scratch[at, :] = all_ref[i, 0:size, :].astype(F32)
                at = slice(out_place * size, (out_place + 1) * size)
                out_ref[at, :] = all_ref[i, size : 2 * size, :].astype(F32)
        in_ref[...] = scratch[...].T

    pl.when(pl.program_id(0) == 0)(lambda: body(0))
    pl.when(pl.program_id(0) == 1)(lambda: body(1))


def assemble(gathered, places, pos, layers, size, base):
    count, _, width = gathered.shape
    chunk = count // 2 * size
    mark = mark_spec()
    return kernel_call(
        functools.partial(assemble_kernel, places, size),
        (2,),
        [pl.BlockSpec(gathered.shape, lambda s: (0, 0, 0))] + free_specs(base),
        [
            pl.BlockSpec((None, width, chunk), lambda s: (pos, 0, s)),
            pl.BlockSpec((None, chunk, width), lambda s: (pos, s, 0)),
            mark[0],
        ],
        [
            jax.ShapeDtypeStruct((layers, width, 2 * chunk), F32),
            jax.ShapeDtypeStruct((layers, 2 * chunk, width), F32),
            mark[1],
        ],
        scratch=[pltpu.VMEM((chunk, width), F32)],
        aliases={1 + i: i for i in range(len(base))},
        cost=cost_of(0, 24 * chunk * width),
    )(gathered, *base)


def mark_kernel(*refs):
    refs[-1][0, 0] = 0.0


def mark_after(*arrays):
    mark = mark_spec()
    return kernel_call(mark_kernel, (1,), free_specs(arrays), mark[0], mark[1])(*arrays)


def norm_block_back(grad, vhat, scale, gain):
    scaled = grad * gain
    inner = (
        scaled
        - jnp.mean(scaled, -1, keepdims=True)
        - vhat * jnp.mean(scaled * vhat, -1, keepdims=True)
    )
    return scale * inner, jnp.sum(grad * vhat, 0, keepdims=True), jnp.sum(grad, 0, keepdims=True)


def token_backward_kernel(
    grad_ref,
    back_ref,
    vhat_two_ref,
    scale_ref,
    act_ref,
    slope_ref,
    low_ref,
    vhat_one_ref,
    norm_ref,
    in_ref,
    out_ref,
    *rest,
):
    next_ref, grads_ref, small_ref, mark_ref = rest[-4:]
    mark_ref[0, 0] = 0.0
    first = pl.program_id(0) == 0

    def add(ref, where, value):
        @pl.when(first)
        def _():
            ref[where] = value

        @pl.when(jnp.logical_not(first))
        def _():
            ref[where] += value

    patches, width = low_ref.shape
    hidden = act_ref.shape[0]
    ones = jnp.ones((8, width), B16)
    pl.when(first)(lambda: small_ref.__setitem__((Ellipsis,), jnp.zeros_like(small_ref)))
    dv, gain_two, shift_two = norm_block_back(
        back_ref[...], vhat_two_ref[...].astype(F32), scale_ref[:, 1:2], norm_ref[1:2, :]
    )
    mid = grad_ref[...].astype(F32) + dv
    low = mid.astype(B16)
    small_ref[5:6, :patches] += dims_nt(ones, low)[0:1, :]
    add(grads_ref, (slice(None), slice(hidden, None)), dims_nt(low, act_ref[...]))
    point = (dims_tn(pad_rows(out_ref[...], patches), low) * slope_ref[...].astype(F32)).astype(B16)
    small_ref[4:5, :hidden] += dims_nt(ones, point)[0:1, :]
    add(grads_ref, (slice(None), slice(0, hidden)), dims_nt(low_ref[...], point))
    dv, gain_one, shift_one = norm_block_back(
        dims_nn(pad_rows(in_ref[...], patches), point),
        vhat_one_ref[...].astype(F32),
        scale_ref[:, 0:1],
        norm_ref[0:1, :],
    )
    next_ref[...] = mid + dv
    for i, value in enumerate((gain_one, gain_two, shift_one, shift_two)):
        small_ref[i : i + 1, :] += value


def token_backward(grad, back, kept, pos, params, images, patches, offset, base, after=()):
    low, act, slope, vhat_one, vhat_two, scale = kept
    norm, w_in, _, w_out, _ = params
    total, width = grad.shape
    hidden = w_in.shape[2]
    rows = images * patches
    block = lambda size, lanes: pl.BlockSpec((size, lanes), lambda i: (i, 0))
    placed = row_block(patches, width, offset)
    shape = lambda r, c: jax.ShapeDtypeStruct((r, c), F32)
    outs = [shape(patches, 2 * hidden), shape(8, width)]
    mark = mark_spec()
    return kernel_call(
        token_backward_kernel,
        (images,),
        [placed, placed, block(patches, width), block(patches, LANES)]
        + [block(hidden, width)] * 2
        + [block(patches, width)] * 2
        + [layer_spec(a, pos) for a in (norm, w_in, w_out)]
        + free_specs(base + after),
        [placed] + [whole_spec(a) for a in outs] + [mark[0]],
        [shape(total, width)] + outs + [mark[1]],
        aliases={11 + i: i for i in range(len(base))},
        cost=cost_of(8 * rows * hidden * width, 30 * rows * width),
    )(grad, back, vhat_two, scale, act, slope, low, vhat_one, norm, w_in, w_out, *base, *after)


def image_split(mesh):
    dp = mesh.shape["dp"]
    return mesh.shape["mp"] == 2 and dp >= 8 and dp & (dp - 1) == 0


def exchange(value, mask, over_mp):
    count = lax.axis_size("dp")
    if not mask:
        return lax.ppermute(value, "mp", [(0, 1), (1, 0)])
    if not over_mp:
        return lax.ppermute(value, "dp", [(i, i ^ mask) for i in range(count)])
    return lax.ppermute(
        value, ("dp", "mp"), [(i, i ^ (2 * mask + 1)) for i in range(2 * count)]
    )


def dp_bit(bit):
    return (lax.axis_index("dp") >> bit) & 1


def join(value, other, flag, axis=0):
    return jnp.where(
        flag == 0,
        jnp.concatenate([value, other], axis),
        jnp.concatenate([other, value], axis),
    )


class Transfers:
    def __init__(self):
        self.flows = []
        self.mark = None

    def start(self, steps, first=False):
        flow = {"steps": steps, "got": None}
        self.flows.insert(0 if first else len(self.flows), flow)
        return flow

    def step(self, flow):
        try:
            if flow["got"] is None:
                sends = next(flow["steps"])
            else:
                sends = flow["steps"].send(flow["got"])
        except StopIteration:
            self.flows.remove(flow)
            return []
        flow["got"] = [exchange(value, *masks) for value, *masks in sends]
        return [send[0] for send in sends]

    def tick(self):
        ties = []
        for flow in list(self.flows):
            ties += self.step(flow)
        return tuple(ties)

    def finish(self, flow):
        self.step(flow)

    def arrived(self):
        self.mark = mark_after(*[got for flow in self.flows for got in flow["got"]])

    def zero(self):
        return self.mark[0, 0]

    def gate(self, value):
        return value if self.mark is None else value + self.zero().astype(value.dtype)

    def add(self, *values):
        total = values[0].astype(F32)
        for value in values[1:]:
            total = total + value.astype(F32)
        return (total + self.zero()).astype(B16)


def one_step(line, value, found, delay=0):
    for _ in range(delay):
        yield []
    (got,) = yield [(line.gate(value), 0, 1)]
    found.append(got)


def fetch_steps(line, weights, pos, found):
    part = dp_bit(0) * 2 + dp_bit(1)
    sends = []
    for weight in weights:
        size = weight.shape[1] // 4
        quarter = lax.dynamic_slice(weight, (pos, part * size, 0), (1, size, weight.shape[2]))
        sends.append(line.gate(quarter))
    near = yield [(s, 0, 1) for s in sends]
    got = yield [(line.gate(s), 2, 0) for s in near]
    pairs = [line.gate(jnp.stack(p)) for p in zip(near, got)]
    far = yield [(s, 1, 0) for s in pairs]
    found += [pairs[0], far[0], pairs[1], far[1]]


def far_blocks(line, value):
    sends = [(value[k], k << 2, 0) for k in range(1, len(value))]
    return value[0], sends


def plain_sum(*values):
    total = values[0].astype(F32)
    for value in values[1:]:
        total = total + value.astype(F32)
    return total.astype(B16)


def upper_grad_steps(line, send, keep, found):
    (got,) = yield [(send, 1, 0)]
    keep = keep[0]
    half = keep.shape[2] // 2
    low, high = slice(half), slice(half, None)
    sum_of = lambda side, blocks: line.add(keep[side, :, blocks], got[side, :, blocks])
    own = [sum_of(1, low), sum_of(1, high)]
    other = [sum_of(0, low), sum_of(0, high)]
    (got,) = yield [(other[1], 0, 1)]
    own[1] = line.add(own[1], got)
    got = yield [(other[0], 0, 1), (own[1], 2, 0)]
    own = line.add(own[0], *got)
    own = jnp.concatenate([own[0], own[1]], 1)
    mine, sends = far_blocks(line, own)
    got = yield sends
    found.append(plain_sum(mine, *got))


def lowest_grad_steps(line, send, keep, found):
    (got,) = yield [(send, 1, 0)]
    keep = keep[0]
    half = keep.shape[2] // 2
    low, high, every = slice(half), slice(half, None), slice(None)
    sum_of = lambda side, item, blocks: line.add(keep[side, item, blocks], got[side, item, blocks])
    in_other, in_low, in_high = sum_of(0, 0, every), sum_of(1, 0, low), sum_of(1, 0, high)
    out_away = sum_of(every, 1, high)
    out_own, out_other = sum_of(1, 1, low), sum_of(0, 1, low)
    got = yield [(in_other, 0, 1), (out_away, 2, 0)]
    in_low, in_high = line.add(in_low, got[0][:half]), line.add(in_high, got[0][half:])
    out_other, out_own = line.add(out_other, got[1][0]), line.add(out_own, got[1][1])
    got = yield [(in_high, 2, 0), (out_other, 0, 1)]
    own = jnp.concatenate([line.add(in_low, got[0]), line.add(out_own, got[1])], 1)
    mine, sends = far_blocks(line, own)
    got = yield sends
    found.append(plain_sum(mine, *got))


def pack_sum_steps(line, pack, at_once, found):
    count = lax.axis_size("dp")
    here = lax.axis_index("dp")
    pack = pack.reshape(count // 4, 2, 2, -1, pack.shape[1])
    near = lambda value, bit, k, axis: lax.dynamic_index_in_dim(value, dp_bit(bit) ^ k, axis, False)
    (got,) = yield [(line.gate(near(pack, 0, 1, 2)), 1, 0)]
    pack = line.add(near(pack, 0, 0, 2), got)
    mine, away = near(pack, 1, 0, 1), near(pack, 1, 1, 1)
    if at_once:
        got = yield [(mine, 0, 1), (away, 2, 0), (away, 2, 1)]
        mine = line.add(mine, *got)
    else:
        (got,) = yield [(away, 2, 0)]
        mine = line.add(mine, got)
        (got,) = yield [(mine, 0, 1)]
        mine = line.add(mine, got)
    far = lambda k: lax.dynamic_index_in_dim(mine, (here >> 2) ^ k, 0, False)
    mine, sends = far_blocks(line, [far(k) for k in range(count // 4)])
    got = yield sends
    found.append(line.add(mine, *got))


def pack_all_steps(line, pack, sums, found):
    mine = []
    yield from pack_sum_steps(line, pack, True, mine)
    mine = jnp.stack(mine + [s[0] for s in sums])
    got = yield [(mine, k << 2, 0) for k in range(1, lax.axis_size("dp") // 4)]
    parts = line.gate(jnp.stack([mine, *got]))
    (got,) = yield [(parts, 2, 0)]
    parts = line.gate(jnp.stack([parts, got], 1))
    (got,) = yield [(parts, 1, 0)]
    parts = jnp.stack([parts, got], 2)
    parts = parts.reshape((-1,) + parts.shape[3:])
    here = lax.axis_index("dp")
    whole = [lax.dynamic_index_in_dim(parts, here ^ k, 0) for k in range(parts.shape[0])]
    found.append(jnp.concatenate(whole))


def block_place(index, bits):
    low = index >> 1
    return (low & 1) << (bits - 2) | low >> 1


def image_body(
    image_small,
    image_large,
    image_counts,
    norm_gain,
    norm_shift,
    mix_in_small,
    mix_bias_small,
    mix_out_small,
    mix_obias_small,
    mix_in_large,
    mix_bias_large,
    mix_out_large,
    mix_obias_large,
    chan_in,
    chan_bias,
    chan_out,
    chan_obias,
    cot_small,
    cot_large,
):
    layers = norm_gain.shape[0]
    own_width = norm_gain.shape[2]
    width = 2 * own_width
    units = chan_bias.shape[1]
    side = lax.axis_index("mp")
    counts = (image_small.shape[0] // 2, image_large.shape[0] // 2)
    patches = (image_small.shape[1], image_large.shape[1])
    padded = tuple(-(-p // 16) * 16 for p in patches)
    offsets = (0, counts[0] * padded[0])

    def pad_patches(field, k, axis):
        widths = [(0, 0)] * field.ndim
        widths[axis] = (0, padded[k] - patches[k])
        return jnp.pad(field, widths)

    def pick(fields, flag):
        parts = []
        for k in range(2):
            part = lax.dynamic_slice_in_dim(fields[k], flag * counts[k], counts[k], 0)
            parts.append(pad_patches(part, k, 1).reshape(-1, own_width))
        return jnp.concatenate(parts, 0)

    def to_features(own, got):
        outs = []
        for k in range(2):
            pair = []
            for v in (own, got):
                v = v[offsets[k] : offsets[k] + counts[k] * padded[k]]
                pair.append(v.reshape(counts[k], padded[k], own_width)[:, : patches[k]])
            outs.append(join(pair[0], pair[1], side, 0))
        return outs

    def features(rows, flag):
        return lax.dynamic_slice_in_dim(rows, flag * own_width, own_width, 1)

    count = lax.axis_size("dp")
    bits = count.bit_length() - 1
    place = block_place(lax.axis_index("dp"), bits)
    info = jnp.stack([side, dp_bit(0), dp_bit(0) * 2 + dp_bit(1), place]).astype(jnp.int32)
    places = [(block_place(i, bits),) * 2 for i in range(count)]

    line = Transfers()
    vectors = jnp.concatenate(
        [norm_gain.reshape(layers, -1), norm_shift.reshape(layers, -1), chan_obias, chan_bias], 1
    )
    live = []
    for k in range(2):
        slot = side * counts[k] + jnp.arange(counts[k], dtype=jnp.int32)
        alive = (slot < image_counts[0, k]).astype(F32)
        live.append(jnp.repeat(alive, padded[k]))
    live = jnp.broadcast_to(jnp.concatenate(live)[:, None], (sum(c * p for c, p in zip(counts, padded)), LANES))
    own = (chan_in, chan_out)
    images = (image_small, image_large)
    cots = (cot_small, cot_large)
    vectors_found, images_found, cot_found, out_found = [], [], [], []
    found = [[] for _ in range(layers)]
    fetches = {0: line.start(fetch_steps(line, own, 0, found[0]))}
    line.tick()
    line.arrived()
    images_flow = line.start(one_step(line, pick(images, 1 - side), images_found))
    vectors_flow = line.start(one_step(line, vectors, vectors_found))
    line.tick()
    line.finish(images_flow)
    line.finish(vectors_flow)
    other_vectors = vectors_found[0]
    line.mark = mark_after(images_found[0])
    if layers > 1:
        fetches[1] = line.start(fetch_steps(line, own, 1, found[1]))
    ties = line.tick()
    stream, line.mark = join_features(
        info, pick(images, side), images_found[0], jnp.ones_like(live)
    )

    mine, theirs = (v[:, : 5 * own_width].reshape(layers, 5, own_width) for v in (vectors, other_vectors))
    whole = join(mine, theirs, side, 2)
    norms, obias_all = whole[:, :4], whole[:, 4:]
    bias_all = jnp.concatenate([chan_bias, other_vectors[:, 5 * own_width :]], 1)[:, None]
    line_of = lambda b: b[:, None, :]
    token_params = (
        (
            norms,
            mix_in_small,
            line_of(mix_bias_small),
            jnp.swapaxes(mix_out_small, 1, 2),
            line_of(mix_obias_small),
        ),
        (
            norms,
            mix_in_large,
            line_of(mix_bias_large),
            jnp.swapaxes(mix_out_large, 1, 2),
            line_of(mix_obias_large),
        ),
    )

    kept = []
    for pos in range(layers):
        if pos > 0:
            if pos == layers - 1:
                line.start(one_step(line, pick(cots, 1 - side), cot_found))
            ties = line.tick()
        parts, base = [], ()
        for k in range(2):
            mixed, rows, *rest, line.mark = token_forward(
                stream, pos, token_params[k], counts[k], padded[k], offsets[k], base, ties
            )
            ties = ()
            base = (mixed, rows)
            parts.append(rest)
        line.finish(fetches[pos])
        if pos + 2 < layers:
            fetches[pos + 2] = line.start(fetch_steps(line, own, pos + 2, found[pos + 2]))
            ties = line.tick()
        quant, slope, stream, *other, line.mark = chan_forward(
            info, rows, mixed, own, found[pos], (pos, 0), bias_all, obias_all, 352, 256, ties
        )
        ties = ()
        kept.append((parts, rows, quant, slope, other))
    if not cot_found:
        if layers == 1:
            line.start(one_step(line, pick(cots, 1 - side), cot_found))
            line.tick()
        line.tick()
    out = (stream * live[:, 0:1]).astype(B16)
    grad, line.mark = join_features(info, pick(cots, side), cot_found[0], live)

    block = units // count
    grads_found = [[] for _ in range(layers)]
    pack_found = [[] for _ in range(layers)]
    gathered = [None] * layers
    chan_grads = ()

    def gather_ready():
        for pos in reversed(range(layers)):
            if gathered[pos] is None and grads_found[pos]:
                payload = grads_found[pos][0]
                if pos + 1 < layers:
                    payload = payload + mark_after(gathered[pos + 1])[0, 0].astype(B16)
                gathered[pos] = lax.all_gather(payload, "dp")

    for pos in reversed(range(layers)):
        parts, rows, quant, slope, other = kept[pos]
        back, small, keep = None, 0.0, []
        for half in range(2):
            ties = line.tick()
            gather_ready()
            value, part_small, back, line.mark = chan_backward(
                info, grad, rows, quant, slope, own, other, pos, back, count // 2, ties
            )
            small = small + part_small
            if half == 0:
                steps = upper_grad_steps if pos > 0 else lowest_grad_steps
                line.start(steps(line, value, keep, grads_found[pos]))
            else:
                keep.append(value)
        ties = line.tick()
        gather_ready()
        base, token_grads, smalls = (), [], []
        for k in range(2):
            following, token_grad, token_small, line.mark = token_backward(
                grad,
                back,
                parts[k],
                pos,
                token_params[k],
                counts[k],
                padded[k],
                offsets[k],
                base,
                ties,
            )
            ties = ()
            base = (following,)
            token_grads.append(token_grad)
            smalls.append(token_small)
        grad = following
        pieces = token_grads + smalls + [small]
        size = sum(p.shape[0] for p in pieces)
        fill = jnp.zeros((-size % (8 * count), width), F32)
        pack = jnp.concatenate(pieces + [fill], 0).astype(B16)
        if pos > 0:
            line.start(pack_sum_steps(line, pack, False, pack_found[pos]), first=True)
        else:
            line.start(pack_all_steps(line, pack, pack_found[1:], pack_found[0]))

    grad_found = []
    line.start(one_step(line, features(grad, 1 - side).astype(B16), grad_found, 2))
    line.start(one_step(line, features(out, 1 - side), out_found, 3))
    done = layers
    while line.flows:
        line.tick()
        gather_ready()
        if done > 1 and (done == layers or gathered[done - 2] is not None):
            done -= 1
            *chan_grads, line.mark = assemble(
                gathered[done], places, done, layers, block, tuple(chan_grads)
            )
        if any(flow["got"] for flow in line.flows):
            line.arrived()
    outs = to_features(features(out, side), out_found[0])
    grads = to_features(features(grad, side), grad_found[0].astype(F32))
    while done:
        done -= 1
        *chan_grads, _ = assemble(gathered[done], places, done, layers, block, tuple(chan_grads))
    pack_rows = pack.shape[0]
    pack = jnp.swapaxes(pack_found[0][0], 0, 1).reshape(layers, pack_rows, width)
    hidden_tok = mix_bias_small.shape[1]
    token_parts = []
    at = 0
    for k in range(2):
        block = pack[:, at : at + patches[k]].astype(F32)
        token_parts.append((block[:, :, :hidden_tok], jnp.swapaxes(block[:, :, hidden_tok:], 1, 2)))
        at += padded[k]
    small = pack[:, at : at + 24].astype(F32)
    mine = lax.dynamic_slice_in_dim(small, side * own_width, own_width, 2)
    norm_g = mine[:, 0:4] + mine[:, 8:12]
    cbias = lax.dynamic_slice_in_dim(small[:, 17:21].reshape(layers, -1), side * units, units, 1)
    return (
        outs[0],
        outs[1],
        grads[0],
        grads[1],
        norm_g[:, 0:2],
        norm_g[:, 2:4],
        token_parts[0][0],
        small[:, 4, :hidden_tok],
        token_parts[0][1],
        small[:, 5, : patches[0]],
        token_parts[1][0],
        small[:, 12, :hidden_tok],
        token_parts[1][1],
        small[:, 13, : patches[1]],
        chan_grads[0],
        cbias,
        chan_grads[1],
        mine[:, 16],
    )


def solution(mesh):
    in_specs = (
        P("dp", None, "mp"),
        P("dp", None, "mp"),
        P("dp", None),
        P(None, None, "mp"),
        P(None, None, "mp"),
        P(),
        P(),
        P(),
        P(),
        P(),
        P(),
        P(),
        P(),
        P(None, None, "mp"),
        P(None, "mp"),
        P(None, "mp", None),
        P(None, "mp"),
        P("dp", None, "mp"),
        P("dp", None, "mp"),
    )
    out_specs = (
        P("dp", None, "mp"),
        P("dp", None, "mp"),
        P("dp", None, "mp"),
        P("dp", None, "mp"),
        P(None, None, "mp"),
        P(None, None, "mp"),
        P(),
        P(),
        P(),
        P(),
        P(),
        P(),
        P(),
        P(),
        P(None, None, "mp"),
        P(None, "mp"),
        P(None, "mp", None),
        P(None, "mp"),
    )
    body = image_body if image_split(mesh) else split_body
    return jax.shard_map(body, mesh=mesh, in_specs=in_specs, out_specs=out_specs, check_vma=False)
```

```python
import functools

import jax
import jax.numpy as jnp
from jax import lax
from jax.experimental import pallas as pl
from jax.experimental.pallas import tpu as pltpu
from jax.sharding import PartitionSpec as P

EPS = 1e-06
F32 = jnp.float32
B16 = jnp.bfloat16


def gelu_exact(field):
    return jax.nn.gelu(field, approximate=False)


def gelu_pull(point, grad_in):
    return jax.vjp(gelu_exact, point)[1](grad_in)[0]


def norm_apply(stream, gain_vec, shift_vec, feature_count):
    totals = lax.psum(
        (
            jnp.sum(stream[0], -1),
            jnp.sum(stream[0] * stream[0], -1),
            jnp.sum(stream[1], -1),
            jnp.sum(stream[1] * stream[1], -1),
        ),
        "mp",
    )
    centred_list, scale_list, normed_list = ([], [], [])
    for set_index in range(2):
        row_mean = totals[2 * set_index] / feature_count
        spread = totals[2 * set_index + 1] / feature_count - row_mean * row_mean
        row_scale = lax.rsqrt(spread + EPS)
        centred = (stream[set_index] - row_mean[..., None]) * row_scale[..., None]
        centred_list.append(centred)
        scale_list.append(row_scale)
        normed_list.append(centred * gain_vec + shift_vec)
    return (centred_list, scale_list, normed_list)


def norm_back(grad_list, centred_list, scale_list, gain_vec, feature_count):
    scaled = [grad_list[0] * gain_vec, grad_list[1] * gain_vec]
    totals = lax.psum(
        (
            jnp.sum(scaled[0], -1),
            jnp.sum(scaled[0] * centred_list[0], -1),
            jnp.sum(scaled[1], -1),
            jnp.sum(scaled[1] * centred_list[1], -1),
        ),
        "mp",
    )
    back_list = []
    for set_index in range(2):
        inner_term = (
            scaled[set_index]
            - totals[2 * set_index][..., None] / feature_count
            - centred_list[set_index] * (totals[2 * set_index + 1][..., None] / feature_count)
        )
        back_list.append(scale_list[set_index][..., None] * inner_term)
    gain_grad = jnp.sum(grad_list[0] * centred_list[0], axis=(0, 1)) + jnp.sum(
        grad_list[1] * centred_list[1], axis=(0, 1)
    )
    shift_grad = jnp.sum(grad_list[0], axis=(0, 1)) + jnp.sum(grad_list[1], axis=(0, 1))
    return (back_list, gain_grad, shift_grad)


def split_body(
    image_small,
    image_large,
    image_counts,
    norm_gain,
    norm_shift,
    mix_in_small,
    mix_bias_small,
    mix_out_small,
    mix_obias_small,
    mix_in_large,
    mix_bias_large,
    mix_out_large,
    mix_obias_large,
    chan_in,
    chan_bias,
    chan_out,
    chan_obias,
    cot_small,
    cot_large,
):
    feature_count = norm_gain.shape[2] * lax.axis_size("mp")
    layers = norm_gain.shape[0]
    slot_count = (image_small.shape[0], image_large.shape[0])
    live_masks = [
        (jnp.arange(slot_count[k], dtype=jnp.int32) < image_counts[0, k]).astype(F32)[:, None, None]
        for k in range(2)
    ]
    mixers = (
        (mix_in_small, mix_bias_small, mix_out_small, mix_obias_small),
        (mix_in_large, mix_bias_large, mix_out_large, mix_obias_large),
    )
    stream = [image_small.astype(F32), image_large.astype(F32)]
    kept_state = []
    for layer_pos in range(layers):
        centred_one, scale_one, normed_one = norm_apply(
            stream, norm_gain[layer_pos, 0], norm_shift[layer_pos, 0], feature_count
        )
        lowered, pre_list, act_list, mixed_list = ([], [], [], [])
        for set_index in range(2):
            token_in, token_bias, token_out, token_obias = mixers[set_index]
            normed_low = normed_one[set_index].astype(B16)
            pre_act = (
                jnp.einsum(
                    "nsc,sh->nhc", normed_low, token_in[layer_pos], preferred_element_type=F32
                )
                + token_bias[layer_pos][None, :, None]
            )
            activated = gelu_exact(pre_act).astype(B16)
            branch = jnp.einsum(
                "nhc,hs->nsc", activated, token_out[layer_pos], preferred_element_type=F32
            )
            mixed_list.append(stream[set_index] + branch + token_obias[layer_pos][None, :, None])
            lowered.append(normed_low)
            pre_list.append(pre_act)
            act_list.append(activated)
        centred_two, scale_two, normed_two = norm_apply(
            mixed_list, norm_gain[layer_pos, 1], norm_shift[layer_pos, 1], feature_count
        )
        normed_rows = (normed_two[0].astype(B16), normed_two[1].astype(B16))
        weight_in = chan_in[layer_pos]
        gathered_rows = None
        hidden = (
            jnp.dot(
                lax.all_gather(normed_rows[0], "mp", axis=2, tiled=True),
                weight_in,
                preferred_element_type=F32,
            ),
            jnp.dot(
                lax.all_gather(normed_rows[1], "mp", axis=2, tiled=True),
                weight_in,
                preferred_element_type=F32,
            ),
        )
        hidden = [hidden[k] + chan_bias[layer_pos] for k in range(2)]
        hidden_low = [gelu_exact(hidden[k]).astype(B16) for k in range(2)]
        partial_value = [
            jnp.dot(hidden_low[k], chan_out[layer_pos], preferred_element_type=F32)
            for k in range(2)
        ]
        summed = (
            lax.psum_scatter(
                partial_value[0].astype(jnp.bfloat16), "mp", scatter_dimension=2, tiled=True
            ).astype(jnp.float32),
            lax.psum_scatter(
                partial_value[1].astype(jnp.bfloat16), "mp", scatter_dimension=2, tiled=True
            ).astype(jnp.float32),
        )
        kept_state.append(
            (
                centred_one,
                scale_one,
                lowered,
                pre_list,
                act_list,
                centred_two,
                scale_two,
                normed_rows,
                gathered_rows,
                hidden,
                hidden_low,
            )
        )
        stream = [mixed_list[k] + summed[k] + chan_obias[layer_pos] for k in range(2)]
    out_list = [(stream[k] * live_masks[k]).astype(B16) for k in range(2)]
    grad_stream = [cot_small.astype(F32) * live_masks[0], cot_large.astype(F32) * live_masks[1]]
    mix_terms = [None] * layers
    chan_terms = [None] * layers
    for layer_pos in reversed(range(layers)):
        (
            centred_one,
            scale_one,
            lowered,
            pre_list,
            act_list,
            centred_two,
            scale_two,
            normed_rows,
            gathered_rows,
            hidden,
            hidden_low,
        ) = kept_state[layer_pos]
        grad_low = (grad_stream[0].astype(B16), grad_stream[1].astype(B16))
        obias_grad = jnp.sum(grad_low[0].astype(F32), axis=(0, 1)) + jnp.sum(
            grad_low[1].astype(F32), axis=(0, 1)
        )
        gathered_grad = (
            lax.all_gather(grad_low[0], "mp", axis=2, tiled=True),
            lax.all_gather(grad_low[1], "mp", axis=2, tiled=True),
        )
        out_grad = jnp.einsum(
            "nsf,nsc->fc", hidden_low[0], gathered_grad[0], preferred_element_type=F32
        ) + jnp.einsum("nsf,nsc->fc", hidden_low[1], gathered_grad[1], preferred_element_type=F32)
        hidden_grad = [
            gelu_pull(
                hidden[k],
                jnp.einsum(
                    "nsc,fc->nsf", gathered_grad[k], chan_out[layer_pos], preferred_element_type=F32
                ),
            ).astype(B16)
            for k in range(2)
        ]
        bias_grad = jnp.sum(hidden_grad[0].astype(F32), axis=(0, 1)) + jnp.sum(
            hidden_grad[1].astype(F32), axis=(0, 1)
        )
        contribution = jnp.einsum(
            "nsk,nsf->kf",
            lax.all_gather(normed_rows[0], "mp", axis=2, tiled=True),
            hidden_grad[0],
            preferred_element_type=F32,
        ) + jnp.einsum(
            "nsk,nsf->kf",
            lax.all_gather(normed_rows[1], "mp", axis=2, tiled=True),
            hidden_grad[1],
            preferred_element_type=F32,
        )
        back_terms = [
            jnp.einsum(
                "nsf,cf->nsc", hidden_grad[k], chan_in[layer_pos], preferred_element_type=F32
            )
            for k in range(2)
        ]
        back_rows = (
            lax.psum_scatter(
                back_terms[0].astype(jnp.bfloat16), "mp", scatter_dimension=2, tiled=True
            ).astype(jnp.float32),
            lax.psum_scatter(
                back_terms[1].astype(jnp.bfloat16), "mp", scatter_dimension=2, tiled=True
            ).astype(jnp.float32),
        )
        norm_grad_two, gain_two, shift_two = norm_back(
            back_rows, centred_two, scale_two, norm_gain[layer_pos, 1], feature_count
        )
        mid_grad = [grad_stream[k] + norm_grad_two[k] for k in range(2)]
        token_terms = []
        norm_input = []
        for set_index in range(2):
            token_in, token_bias, token_out, token_obias = mixers[set_index]
            token_grad = mid_grad[set_index].astype(B16)
            token_obias_grad = jnp.sum(token_grad.astype(F32), axis=(0, 2))
            token_out_grad = jnp.einsum(
                "nhc,nsc->hs", act_list[set_index], token_grad, preferred_element_type=F32
            )
            act_grad = jnp.einsum(
                "nsc,hs->nhc", token_grad, token_out[layer_pos], preferred_element_type=F32
            )
            pre_grad = gelu_pull(pre_list[set_index], act_grad).astype(B16)
            token_bias_grad = jnp.sum(pre_grad.astype(F32), axis=(0, 2))
            token_in_grad = jnp.einsum(
                "nsc,nhc->sh", lowered[set_index], pre_grad, preferred_element_type=F32
            )
            norm_input.append(
                jnp.einsum("nhc,sh->nsc", pre_grad, token_in[layer_pos], preferred_element_type=F32)
            )
            token_terms += [token_in_grad, token_bias_grad, token_out_grad, token_obias_grad]
        norm_grad_one, gain_one, shift_one = norm_back(
            norm_input, centred_one, scale_one, norm_gain[layer_pos, 0], feature_count
        )
        grad_stream = [mid_grad[k] + norm_grad_one[k] for k in range(2)]
        chan_local = (
            contribution,
            bias_grad,
            out_grad,
            obias_grad,
            jnp.stack([gain_one, gain_two]),
            jnp.stack([shift_one, shift_two]),
        )
        mix_terms[layer_pos] = lax.psum(
            (
                token_terms[0],
                token_terms[1],
                token_terms[2],
                token_terms[3],
                token_terms[4],
                token_terms[5],
                token_terms[6],
                token_terms[7],
            ),
            ("dp", "mp"),
        )
        chan_terms[layer_pos] = (
            lax.psum(chan_local[0].astype(jnp.bfloat16), "dp").astype(jnp.float32),
            lax.psum(chan_local[1].astype(jnp.bfloat16), "dp").astype(jnp.float32),
            lax.psum(chan_local[2].astype(jnp.bfloat16), "dp").astype(jnp.float32),
            lax.psum(chan_local[3].astype(jnp.bfloat16), "dp").astype(jnp.float32),
            lax.psum(chan_local[4].astype(jnp.bfloat16), "dp").astype(jnp.float32),
            lax.psum(chan_local[5].astype(jnp.bfloat16), "dp").astype(jnp.float32),
        )
    mix_stacked = [jnp.stack([mix_terms[pos][item] for pos in range(layers)]) for item in range(8)]
    chan_stacked = [
        jnp.stack([chan_terms[pos][item] for pos in range(layers)]) for item in range(6)
    ]
    return (
        out_list[0],
        out_list[1],
        grad_stream[0],
        grad_stream[1],
        chan_stacked[4],
        chan_stacked[5],
        mix_stacked[0],
        mix_stacked[1],
        mix_stacked[2],
        mix_stacked[3],
        mix_stacked[4],
        mix_stacked[5],
        mix_stacked[6],
        mix_stacked[7],
        chan_stacked[0],
        chan_stacked[1],
        chan_stacked[2],
        chan_stacked[3],
    )


LANES = 128
SIDE, CORE, QUARTER, PLACE = range(4)
VMEM_LIMIT = 56 << 20
COST_SCALE = 200


def gelu_pair(point):
    below = 0.5 + 0.5 * lax.erf(point * 0.7071067811865476)
    bell = jnp.exp(point * point * -0.5) * 0.3989422804014327
    return point * below, below + point * bell


def kernel_call(
    kernel, grid, in_specs, out_specs, out_shape, scratch=(), cost=None, aliases=None, prefetch=0
):
    return pl.pallas_call(
        kernel,
        grid_spec=pltpu.PrefetchScalarGridSpec(
            num_scalar_prefetch=prefetch,
            grid=grid,
            in_specs=in_specs,
            out_specs=out_specs,
            scratch_shapes=list(scratch),
        ),
        out_shape=out_shape,
        compiler_params=pltpu.CompilerParams(vmem_limit_bytes=VMEM_LIMIT),
        cost_estimate=cost,
        input_output_aliases=aliases or {},
    )


def cost_of(flops, nbytes):
    return pl.CostEstimate(
        flops=int(COST_SCALE * flops), bytes_accessed=int(COST_SCALE * nbytes), transcendentals=0
    )


def mark_spec():
    return pl.BlockSpec(memory_space=pltpu.SMEM), jax.ShapeDtypeStruct((1, 1), F32)


def column(row, size):
    pad = -row.shape[1] % LANES
    if pad:
        row = jnp.concatenate([row, jnp.zeros((1, pad), F32)], 1)
    return jnp.broadcast_to(row, (8, row.shape[1])).T[:size, 0:1]


def pad_rows(value, size):
    if value.shape[0] == size:
        return value
    return jnp.concatenate([value, jnp.zeros((size - value.shape[0], value.shape[1]), value.dtype)], 0)


def dims_nt(left, right):
    return lax.dot_general(left, right, (((1,), (1,)), ((), ())), preferred_element_type=F32)


def dims_tn(left, right):
    return lax.dot_general(left, right, (((0,), (0,)), ((), ())), preferred_element_type=F32)


def dims_nn(left, right):
    return jnp.dot(left, right, preferred_element_type=F32)


def norm_block(field):
    centred = field - jnp.mean(field, -1, keepdims=True)
    scale = lax.rsqrt(jnp.mean(centred * centred, -1, keepdims=True) + EPS)
    return centred * scale, scale


def token_forward_kernel(x_ref, norm_ref, in_ref, bias_ref, out_ref, obias_ref, *rest):
    (
        mixed_ref,
        rows_ref,
        low_ref,
        act_ref,
        slope_ref,
        vhat_one_ref,
        vhat_two_ref,
        scale_ref,
        mark_ref,
    ) = rest[-9:]
    x = x_ref[...]
    size = x.shape[0]
    vhat, scale = norm_block(x)
    vhat_one_ref[...] = vhat.astype(B16)
    low = (vhat * norm_ref[0:1, :] + norm_ref[2:3, :]).astype(B16)
    low_ref[...] = low
    point = dims_tn(pad_rows(in_ref[...], size), low) + column(bias_ref[...], act_ref.shape[0])
    act, slope = gelu_pair(point)
    act = act.astype(B16)
    act_ref[...] = act
    slope_ref[...] = slope.astype(B16)
    mixed = x + dims_nn(pad_rows(out_ref[...], size), act) + column(obias_ref[...], size)
    mixed_ref[...] = mixed
    vhat, scale_two = norm_block(mixed)
    vhat_two_ref[...] = vhat.astype(B16)
    rows_ref[...] = (vhat * norm_ref[1:2, :] + norm_ref[3:4, :]).astype(B16)
    scale_ref[:, 0:1] = scale
    scale_ref[:, 1:2] = scale_two
    mark_ref[0, 0] = 0.0


def row_block(patches, width, offset):
    return pl.BlockSpec(
        (pl.Element(patches), pl.Element(width)),
        lambda i: ((offset // 16 + i * (patches // 16)) * 16, 0),
    )


def whole_spec(array):
    return pl.BlockSpec(array.shape, lambda *i: (0, 0))


def free_specs(arrays):
    return [pl.BlockSpec(memory_space=pl.ANY)] * len(arrays)


def layer_spec(array, pos):
    return pl.BlockSpec(
        (None,) + array.shape[1:], lambda *i: (pos,) + (0,) * (array.ndim - 1)
    )


def token_forward(x, pos, params, images, patches, offset, base, after=()):
    total, width = x.shape
    hidden = params[1].shape[2]
    rows = images * patches
    block = lambda size, lanes: pl.BlockSpec((size, lanes), lambda i: (i, 0))
    placed = row_block(patches, width, offset)
    shape = jax.ShapeDtypeStruct
    mark = mark_spec()
    return kernel_call(
        token_forward_kernel,
        (images,),
        [placed] + [layer_spec(a, pos) for a in params] + free_specs(base + after),
        [placed, placed]
        + [block(patches, width)]
        + [block(hidden, width)] * 2
        + [block(patches, width)] * 2
        + [block(patches, LANES), mark[0]],
        [
            shape((total, width), F32),
            shape((total, width), B16),
            shape((rows, width), B16),
            shape((images * hidden, width), B16),
            shape((images * hidden, width), B16),
            shape((rows, width), B16),
            shape((rows, width), B16),
            shape((rows, LANES), F32),
            mark[1],
        ],
        aliases={6 + i: i for i in range(len(base))},
        cost=cost_of(4 * rows * hidden * width, 30 * rows * width),
    )(x, *params, *base, *after)


def join_kernel(info_ref, own_ref, got_ref, live_ref, joined_ref, mark_ref):
    own, got = own_ref[...].astype(F32), got_ref[...].astype(F32)
    first = info_ref[SIDE] == 0
    live = live_ref[:, 0:1]
    half = own.shape[1]
    joined_ref[:, :half] = jnp.where(first, own, got) * live
    joined_ref[:, half:] = jnp.where(first, got, own) * live
    mark_ref[0, 0] = 0.0


def join_features(info, own, got, live, tiles=4):
    rows, half = own.shape
    block = lambda lanes: pl.BlockSpec((rows // tiles, lanes), lambda i, _: (i, 0))
    mark = mark_spec()
    return kernel_call(
        join_kernel,
        (tiles,),
        [block(half), block(half), block(LANES)],
        [block(2 * half), mark[0]],
        [jax.ShapeDtypeStruct((rows, 2 * half), F32), mark[1]],
        prefetch=1,
        cost=cost_of(0, 12 * rows * half),
    )(info, own, got, live)


def chan_forward_kernel(
    part,
    info_ref,
    rows_ref,
    mixed_ref,
    in_own_ref,
    out_own_ref,
    in_near_ref,
    in_far_ref,
    out_near_ref,
    out_far_ref,
    bias_ref,
    obias_ref,
    *rest,
):
    quant_ref, slope_ref, total_ref, in_other_ref, out_other_ref, mark_ref = rest[-6:]
    mark_ref[0, 0] = 0.0

    @pl.when(pl.program_id(0) == 0)
    def _():
        place = info_ref[QUARTER]
        for pieces, other_ref in (
            ((in_near_ref, in_far_ref), in_other_ref),
            ((out_near_ref, out_far_ref), out_other_ref),
        ):
            size = pieces[0].shape[1]
            for k in range(4):
                at = pl.multiple_of((place ^ k) * size, size)
                other_ref[pl.ds(at, size), :] = pieces[k // 2][k % 2]

    rows = rows_ref[...]
    total = mixed_ref[...] + obias_ref[...]
    units = in_own_ref.shape[1]
    for side, (in_ref, out_ref) in enumerate(
        ((in_own_ref, out_own_ref), (in_other_ref, out_other_ref))
    ):
        for at in range(0, units, part):
            lanes = slice(at, at + part)
            place = slice(side * units + at, side * units + at + part)
            point = dims_nn(rows, in_ref[:, lanes]) + bias_ref[:, place]
            quant, slope = gelu_pair(point)
            quant = quant.astype(B16)
            quant_ref[:, place] = quant
            slope_ref[:, place] = slope.astype(B16)
            total = total + dims_nn(quant, out_ref[lanes, :])
    total_ref[...] = total


def chan_forward(info, rows, mixed, own, found, layer, bias, obias, tile, part, after=()):
    pos, at = layer
    count, width = rows.shape
    units = bias.shape[2]
    half = units // 2
    mark = mark_spec()
    tiled = pl.BlockSpec((tile, width), lambda i, _: (i, 0))
    lanes = pl.BlockSpec((tile, units), lambda i, _: (i, 0))
    once = lambda rows, cols: pl.BlockSpec((rows, cols), lambda i, _: (0, 0))
    layered = lambda a: pl.BlockSpec((None,) + a.shape[1:], lambda i, _: (pos, 0, 0))
    pieces = lambda a: pl.BlockSpec(
        (a.shape[0], None) + a.shape[2:], lambda i, _: (0, at, 0, 0)
    )
    return kernel_call(
        functools.partial(chan_forward_kernel, part),
        (count // tile,),
        [tiled, tiled]
        + [layered(a) for a in own]
        + [pieces(a) for a in found]
        + [layered(bias), layered(obias)]
        + free_specs(after),
        [lanes, lanes, tiled, once(width, half), once(half, width), mark[0]],
        [
            jax.ShapeDtypeStruct((count, units), B16),
            jax.ShapeDtypeStruct((count, units), B16),
            jax.ShapeDtypeStruct((count, width), F32),
            jax.ShapeDtypeStruct((width, half), B16),
            jax.ShapeDtypeStruct((half, width), B16),
            mark[1],
        ],
        prefetch=1,
        cost=cost_of(4 * count * units * width, 4 * count * units + 10 * count * width),
    )(info, rows, mixed, *own, *found, bias, obias, *after)


def chan_backward_kernel(
    blocks,
    halves,
    info_ref,
    grad_ref,
    rows_ref,
    quant_ref,
    slope_ref,
    in_own_ref,
    out_own_ref,
    in_other_ref,
    out_other_ref,
    *rest,
):
    *sum_refs, small_ref, back_ref, mark_ref, low_ref = rest[-4 - len(halves) :]
    mark_ref[0, 0] = 0.0
    step = pl.program_id(0)

    @pl.when(step == 0)
    def _():
        low = grad_ref[...].astype(B16)
        low_ref[...] = low
        small_ref[...] = jnp.zeros_like(small_ref)
        if halves[0] == 0:
            small_ref[0:1, :] = jnp.sum(low.astype(F32), 0, keepdims=True)
            back_ref[...] = jnp.zeros_like(back_ref)
        else:
            back_ref[...] = rest[0][...]

    def body(other, keep, in_ref, out_ref, sum_ref):
        low = low_ref[...]
        hidden = (dims_nt(low, out_ref[...]) * slope_ref[...].astype(F32)).astype(B16)
        core = info_ref[CORE] if keep else 1 - info_ref[CORE]
        row = 1 + 2 * (info_ref[SIDE] ^ other) + core
        small_ref[pl.ds(row, 1), :] = jnp.sum(hidden.astype(F32), 0, keepdims=True)
        for item, grads in enumerate(
            (dims_tn(hidden, rows_ref[...]), dims_tn(quant_ref[...], low))
        ):
            size = grads.shape[0] // blocks
            for k in range(blocks):
                part = grads[k * size : (k + 1) * size, :].astype(B16)
                sum_ref[item, k ^ info_ref[PLACE]] = part
        back_ref[...] += dims_nt(hidden, in_ref[...])

    sides = ((in_own_ref, out_own_ref), (in_other_ref, out_other_ref))
    for k in range(2 * len(halves)):
        other, place = 1 - k % 2, k // 2

        @pl.when(step == k)
        def _(other=other, place=place):
            body(other, halves[place], *sides[other], sum_refs[place])


def chan_backward(
    info, grad, rows, quant, slope, own, other, pos, back, blocks, halves, after=()
):
    count, width = rows.shape
    chunk = own[0].shape[2] // 2
    if len(halves) == 2:
        core = lambda s, info: jnp.where(s < 2, 1 - info[CORE], info[CORE])
        which = lambda s: (jnp.minimum(s, 1), jnp.maximum(s - 2, 0))
    else:
        core = lambda s, info: info[CORE] if halves[0] else 1 - info[CORE]
        which = lambda s: (s,)
    lanes = pl.BlockSpec(
        (count, chunk), lambda s, info: (0, 2 * (1 - lax.rem(s, 2)) + core(s, info))
    )
    once = lambda rows, cols: pl.BlockSpec((rows, cols), lambda s, _: (0, 0))
    part = (None, 2, blocks, chunk // blocks, width)
    sums = [
        pl.BlockSpec(part, lambda s, _, i=i: (which(s)[i], 0, 0, 0, 0))
        for i in range(len(halves))
    ]
    extra = () if halves[0] == 0 else (back,)
    mark = mark_spec()
    return kernel_call(
        functools.partial(chan_backward_kernel, blocks, halves),
        (2 * len(halves),),
        [once(count, width), once(count, width), lanes, lanes]
        + [
            pl.BlockSpec((None, width, chunk), lambda s, info: (pos, 0, core(s, info))),
            pl.BlockSpec((None, chunk, width), lambda s, info: (pos, core(s, info), 0)),
            pl.BlockSpec((width, chunk), lambda s, info: (0, core(s, info))),
            pl.BlockSpec((chunk, width), lambda s, info: (core(s, info), 0)),
        ]
        + [once(count, width)] * len(extra)
        + free_specs(after),
        sums + [once(8, width), once(count, width), mark[0]],
        [jax.ShapeDtypeStruct((2,) + part[1:], B16)] * len(halves)
        + [
            jax.ShapeDtypeStruct((8, width), F32),
            jax.ShapeDtypeStruct((count, width), F32),
            mark[1],
        ],
        scratch=[pltpu.VMEM((count, width), B16)],
        prefetch=1,
        cost=cost_of(
            16 * len(halves) * count * chunk * width, 8 * count * chunk + 16 * count * width
        ),
    )(info, grad, rows, quant, slope, *own, *other, *extra, *after)


def assemble_kernel(places, size, all_ref, *rest):
    in_ref, out_ref, mark_ref, scratch = rest[-4:]
    mark_ref[0, 0] = 0.0

    def body(core):
        for i, (in_place, out_place) in enumerate(places):
            if i % 2 == core:
                at = slice(in_place * size, (in_place + 1) * size)
                scratch[at, :] = all_ref[i, 0:size, :].astype(F32)
                at = slice(out_place * size, (out_place + 1) * size)
                out_ref[at, :] = all_ref[i, size : 2 * size, :].astype(F32)
        in_ref[...] = scratch[...].T

    pl.when(pl.program_id(0) == 0)(lambda: body(0))
    pl.when(pl.program_id(0) == 1)(lambda: body(1))


def assemble(gathered, places, pos, layers, size, base):
    count, _, width = gathered.shape
    chunk = count // 2 * size
    mark = mark_spec()
    return kernel_call(
        functools.partial(assemble_kernel, places, size),
        (2,),
        [pl.BlockSpec(gathered.shape, lambda s: (0, 0, 0))] + free_specs(base),
        [
            pl.BlockSpec((None, width, chunk), lambda s: (pos, 0, s)),
            pl.BlockSpec((None, chunk, width), lambda s: (pos, s, 0)),
            mark[0],
        ],
        [
            jax.ShapeDtypeStruct((layers, width, 2 * chunk), F32),
            jax.ShapeDtypeStruct((layers, 2 * chunk, width), F32),
            mark[1],
        ],
        scratch=[pltpu.VMEM((chunk, width), F32)],
        aliases={1 + i: i for i in range(len(base))},
        cost=cost_of(0, 24 * chunk * width),
    )(gathered, *base)


def mark_kernel(*refs):
    refs[-1][0, 0] = 0.0


def mark_after(*arrays):
    mark = mark_spec()
    return kernel_call(mark_kernel, (1,), free_specs(arrays), mark[0], mark[1])(*arrays)


def norm_block_back(grad, vhat, scale, gain):
    scaled = grad * gain
    inner = (
        scaled
        - jnp.mean(scaled, -1, keepdims=True)
        - vhat * jnp.mean(scaled * vhat, -1, keepdims=True)
    )
    return scale * inner, jnp.sum(grad * vhat, 0, keepdims=True), jnp.sum(grad, 0, keepdims=True)


def token_backward_kernel(
    grad_ref,
    back_ref,
    vhat_two_ref,
    scale_ref,
    act_ref,
    slope_ref,
    low_ref,
    vhat_one_ref,
    norm_ref,
    in_ref,
    out_ref,
    *rest,
):
    next_ref, grads_ref, small_ref, mark_ref = rest[-4:]
    mark_ref[0, 0] = 0.0
    first = pl.program_id(0) == 0

    def add(ref, where, value):
        @pl.when(first)
        def _():
            ref[where] = value

        @pl.when(jnp.logical_not(first))
        def _():
            ref[where] += value

    patches, width = low_ref.shape
    hidden = act_ref.shape[0]
    ones = jnp.ones((8, width), B16)
    pl.when(first)(lambda: small_ref.__setitem__((Ellipsis,), jnp.zeros_like(small_ref)))
    dv, gain_two, shift_two = norm_block_back(
        back_ref[...], vhat_two_ref[...].astype(F32), scale_ref[:, 1:2], norm_ref[1:2, :]
    )
    mid = grad_ref[...].astype(F32) + dv
    low = mid.astype(B16)
    small_ref[5:6, :patches] += dims_nt(ones, low)[0:1, :]
    add(grads_ref, (slice(None), slice(hidden, None)), dims_nt(low, act_ref[...]))
    point = (dims_tn(pad_rows(out_ref[...], patches), low) * slope_ref[...].astype(F32)).astype(B16)
    small_ref[4:5, :hidden] += dims_nt(ones, point)[0:1, :]
    add(grads_ref, (slice(None), slice(0, hidden)), dims_nt(low_ref[...], point))
    dv, gain_one, shift_one = norm_block_back(
        dims_nn(pad_rows(in_ref[...], patches), point),
        vhat_one_ref[...].astype(F32),
        scale_ref[:, 0:1],
        norm_ref[0:1, :],
    )
    next_ref[...] = mid + dv
    for i, value in enumerate((gain_one, gain_two, shift_one, shift_two)):
        small_ref[i : i + 1, :] += value


def token_backward(grad, back, kept, pos, params, images, patches, offset, base, after=()):
    low, act, slope, vhat_one, vhat_two, scale = kept
    norm, w_in, _, w_out, _ = params
    total, width = grad.shape
    hidden = w_in.shape[2]
    rows = images * patches
    block = lambda size, lanes: pl.BlockSpec((size, lanes), lambda i: (i, 0))
    placed = row_block(patches, width, offset)
    shape = lambda r, c: jax.ShapeDtypeStruct((r, c), F32)
    outs = [shape(patches, 2 * hidden), shape(8, width)]
    mark = mark_spec()
    return kernel_call(
        token_backward_kernel,
        (images,),
        [placed, placed, block(patches, width), block(patches, LANES)]
        + [block(hidden, width)] * 2
        + [block(patches, width)] * 2
        + [layer_spec(a, pos) for a in (norm, w_in, w_out)]
        + free_specs(base + after),
        [placed] + [whole_spec(a) for a in outs] + [mark[0]],
        [shape(total, width)] + outs + [mark[1]],
        aliases={11 + i: i for i in range(len(base))},
        cost=cost_of(8 * rows * hidden * width, 30 * rows * width),
    )(grad, back, vhat_two, scale, act, slope, low, vhat_one, norm, w_in, w_out, *base, *after)


def image_split(mesh):
    dp = mesh.shape["dp"]
    return mesh.shape["mp"] == 2 and dp >= 8 and dp & (dp - 1) == 0


def exchange(value, mask, over_mp):
    count = lax.axis_size("dp")
    if not mask:
        return lax.ppermute(value, "mp", [(0, 1), (1, 0)])
    if not over_mp:
        return lax.ppermute(value, "dp", [(i, i ^ mask) for i in range(count)])
    return lax.ppermute(
        value, ("dp", "mp"), [(i, i ^ (2 * mask + 1)) for i in range(2 * count)]
    )


def dp_bit(bit):
    return (lax.axis_index("dp") >> bit) & 1


def join(value, other, flag, axis=0):
    return jnp.where(
        flag == 0,
        jnp.concatenate([value, other], axis),
        jnp.concatenate([other, value], axis),
    )


class Transfers:
    def __init__(self):
        self.flows = []
        self.mark = None

    def start(self, steps, first=False, tied=False):
        flow = {"steps": steps, "got": None, "tied": tied}
        self.flows.insert(0 if first else len(self.flows), flow)
        return flow

    def step(self, flow):
        try:
            if flow["got"] is None:
                sends = next(flow["steps"])
            else:
                sends = flow["steps"].send(flow["got"])
        except StopIteration:
            self.flows.remove(flow)
            return list(flow["got"]) if flow["tied"] else []
        flow["got"] = [exchange(value, *masks) for value, *masks in sends]
        return [send[0] for send in sends]

    def tick(self):
        ties = []
        for flow in list(self.flows):
            ties += self.step(flow)
        return tuple(ties)

    def finish(self, flow):
        self.step(flow)

    def arrived(self, *also):
        self.mark = mark_after(*[got for flow in self.flows for got in flow["got"]], *also)

    def zero(self):
        return self.mark[0, 0]

    def gate(self, value):
        return value if self.mark is None else value + self.zero().astype(value.dtype)

    def add(self, *values):
        total = values[0].astype(F32)
        for value in values[1:]:
            total = total + value.astype(F32)
        return (total + self.zero()).astype(B16)


def one_step(line, value, found, delay=0):
    for _ in range(delay):
        yield []
    (got,) = yield [(line.gate(value), 0, 1)]
    found.append(got)


def fetch_steps(line, weights, pos, found):
    part = dp_bit(0) * 2 + dp_bit(1)
    sends = []
    for weight in weights:
        size = weight.shape[1] // 4
        quarter = lax.dynamic_slice(weight, (pos, part * size, 0), (1, size, weight.shape[2]))
        sends.append(line.gate(quarter))
    near = yield [(s, 0, 1) for s in sends]
    got = yield [(line.gate(s), 2, 0) for s in near]
    pairs = [line.gate(jnp.stack(p)) for p in zip(near, got)]
    far = yield [(s, 1, 0) for s in pairs]
    found += [pairs[0], far[0], pairs[1], far[1]]


def far_blocks(line, value):
    sends = [(value[k], k << 2, 0) for k in range(1, len(value))]
    return value[0], sends


def plain_sum(*values):
    total = values[0].astype(F32)
    for value in values[1:]:
        total = total + value.astype(F32)
    return total.astype(B16)


def upper_grad_steps(line, send, keep, pack, found):
    (got,) = yield [(send, 1, 0)]
    keep = keep[0]
    half = keep.shape[2] // 2
    low, high = slice(half), slice(half, None)
    sum_of = lambda side, blocks: line.add(keep[side, :, blocks], got[side, :, blocks])
    own = [sum_of(1, low), sum_of(1, high)]
    other = [sum_of(0, low), sum_of(0, high)]
    (got,) = yield [(other[1], 0, 1)]
    own[1] = line.add(own[1], got)
    got = yield [(other[0], 0, 1), (own[1], 2, 0)]
    own = line.add(own[0], *got)
    own = jnp.concatenate([own[0], own[1], *pack], 1)
    mine, sends = far_blocks(line, own)
    got = yield sends
    found.append(plain_sum(mine, *got))


def lowest_grad_steps(line, send, keep, pack, found):
    (got,) = yield [(send, 1, 0)]
    keep = keep[0]
    half = keep.shape[2] // 2
    low, high, every = slice(half), slice(half, None), slice(None)
    sum_of = lambda side, item, blocks: line.add(keep[side, item, blocks], got[side, item, blocks])
    in_other, in_low, in_high = sum_of(0, 0, every), sum_of(1, 0, low), sum_of(1, 0, high)
    out_away = sum_of(every, 1, high)
    out_own, out_other = sum_of(1, 1, low), sum_of(0, 1, low)
    got = yield [(in_other, 0, 1), (out_away, 2, 0)]
    in_low, in_high = line.add(in_low, got[0][:half]), line.add(in_high, got[0][half:])
    out_other, out_own = line.add(out_other, got[1][0]), line.add(out_own, got[1][1])
    got = yield [(in_high, 2, 0), (out_other, 0, 1)]
    own = jnp.concatenate([line.add(in_low, got[0]), line.add(out_own, got[1]), *pack], 1)
    mine, sends = far_blocks(line, own)
    got = yield sends
    found.append(line.add(mine, *got))


def pack_near_steps(line, pack, found):
    count = lax.axis_size("dp")
    here = lax.axis_index("dp")
    pack = pack.reshape(count // 4, 2, 2, -1, pack.shape[1])
    near = lambda value, bit, k, axis: lax.dynamic_index_in_dim(value, dp_bit(bit) ^ k, axis, False)
    (got,) = yield [(line.gate(near(pack, 0, 1, 2)), 1, 0)]
    pack = line.add(near(pack, 0, 0, 2), got)
    (got,) = yield [(near(pack, 1, 1, 1), 2, 0)]
    mine = line.add(near(pack, 1, 0, 1), got)
    (got,) = yield [(mine, 0, 1)]
    mine = line.add(mine, got)
    far = lambda k: lax.dynamic_index_in_dim(mine, (here >> 2) ^ k, 0, False)
    found.append(jnp.stack([far(k) for k in range(count // 4)]))


def pack_all_steps(line, pack, found):
    near = []
    yield from pack_near_steps(line, pack, near)
    mine, sends = far_blocks(line, near[0])
    got = yield sends
    mine = line.add(mine, *got)
    got = yield [(mine, k << 2, 0) for k in range(1, lax.axis_size("dp") // 4)]
    parts = line.gate(jnp.stack([mine, *got]))
    (got,) = yield [(parts, 2, 0)]
    parts = line.gate(jnp.stack([parts, got], 1))
    (got,) = yield [(parts, 1, 0)]
    parts = jnp.stack([parts, got], 2)
    parts = parts.reshape((-1,) + parts.shape[3:])
    here = lax.axis_index("dp")
    whole = [lax.dynamic_index_in_dim(parts, here ^ k, 0) for k in range(parts.shape[0])]
    found.append(jnp.concatenate(whole))


def block_place(index, bits):
    low = index >> 1
    return (low & 1) << (bits - 2) | low >> 1


def image_body(
    image_small,
    image_large,
    image_counts,
    norm_gain,
    norm_shift,
    mix_in_small,
    mix_bias_small,
    mix_out_small,
    mix_obias_small,
    mix_in_large,
    mix_bias_large,
    mix_out_large,
    mix_obias_large,
    chan_in,
    chan_bias,
    chan_out,
    chan_obias,
    cot_small,
    cot_large,
):
    layers = norm_gain.shape[0]
    own_width = norm_gain.shape[2]
    width = 2 * own_width
    units = chan_bias.shape[1]
    side = lax.axis_index("mp")
    counts = (image_small.shape[0] // 2, image_large.shape[0] // 2)
    patches = (image_small.shape[1], image_large.shape[1])
    padded = tuple(-(-p // 16) * 16 for p in patches)
    offsets = (0, counts[0] * padded[0])

    def pad_patches(field, k, axis):
        widths = [(0, 0)] * field.ndim
        widths[axis] = (0, padded[k] - patches[k])
        return jnp.pad(field, widths)

    def pick(fields, flag):
        parts = []
        for k in range(2):
            part = lax.dynamic_slice_in_dim(fields[k], flag * counts[k], counts[k], 0)
            parts.append(pad_patches(part, k, 1).reshape(-1, own_width))
        return jnp.concatenate(parts, 0)

    def to_features(own, got):
        outs = []
        for k in range(2):
            pair = []
            for v in (own, got):
                v = v[offsets[k] : offsets[k] + counts[k] * padded[k]]
                pair.append(v.reshape(counts[k], padded[k], own_width)[:, : patches[k]])
            outs.append(join(pair[0], pair[1], side, 0))
        return outs

    def features(rows, flag):
        return lax.dynamic_slice_in_dim(rows, flag * own_width, own_width, 1)

    count = lax.axis_size("dp")
    bits = count.bit_length() - 1
    place = block_place(lax.axis_index("dp"), bits)
    info = jnp.stack([side, dp_bit(0), dp_bit(0) * 2 + dp_bit(1), place]).astype(jnp.int32)
    places = [(block_place(i, bits),) * 2 for i in range(count)]

    line = Transfers()
    vectors = jnp.concatenate(
        [norm_gain.reshape(layers, -1), norm_shift.reshape(layers, -1), chan_obias, chan_bias], 1
    )
    live = []
    for k in range(2):
        slot = side * counts[k] + jnp.arange(counts[k], dtype=jnp.int32)
        alive = (slot < image_counts[0, k]).astype(F32)
        live.append(jnp.repeat(alive, padded[k]))
    live = jnp.broadcast_to(jnp.concatenate(live)[:, None], (sum(c * p for c, p in zip(counts, padded)), LANES))
    own = (chan_in, chan_out)
    images = (image_small, image_large)
    cots = (cot_small, cot_large)
    vectors_found, images_found, cot_found, out_found = [], [], [], []
    found = [[] for _ in range(layers)]
    fetches = {0: line.start(fetch_steps(line, own, 0, found[0]))}
    line.tick()
    line.arrived()
    images_flow = line.start(one_step(line, pick(images, 1 - side), images_found))
    vectors_flow = line.start(one_step(line, vectors, vectors_found))
    line.tick()
    line.finish(images_flow)
    line.finish(vectors_flow)
    other_vectors = vectors_found[0]
    line.mark = mark_after(images_found[0])
    if layers > 1:
        fetches[1] = line.start(fetch_steps(line, own, 1, found[1]))
    ties = line.tick()
    stream, line.mark = join_features(
        info, pick(images, side), images_found[0], jnp.ones_like(live)
    )

    mine, theirs = (v[:, : 5 * own_width].reshape(layers, 5, own_width) for v in (vectors, other_vectors))
    whole = join(mine, theirs, side, 2)
    norms, obias_all = whole[:, :4], whole[:, 4:]
    bias_all = jnp.concatenate([chan_bias, other_vectors[:, 5 * own_width :]], 1)[:, None]
    line_of = lambda b: b[:, None, :]
    token_params = (
        (
            norms,
            mix_in_small,
            line_of(mix_bias_small),
            jnp.swapaxes(mix_out_small, 1, 2),
            line_of(mix_obias_small),
        ),
        (
            norms,
            mix_in_large,
            line_of(mix_bias_large),
            jnp.swapaxes(mix_out_large, 1, 2),
            line_of(mix_obias_large),
        ),
    )

    kept = []
    for pos in range(layers):
        if pos > 0:
            if pos == 1:
                line.start(one_step(line, pick(cots, 1 - side), cot_found))
            ties = line.tick()
        parts, base = [], ()
        for k in range(2):
            mixed, rows, *rest, line.mark = token_forward(
                stream, pos, token_params[k], counts[k], padded[k], offsets[k], base, ties
            )
            ties = ()
            base = (mixed, rows)
            parts.append(rest)
        line.finish(fetches[pos])
        if pos + 2 < layers:
            fetches[pos + 2] = line.start(fetch_steps(line, own, pos + 2, found[pos + 2]))
            ties = line.tick()
        quant, slope, stream, *other, line.mark = chan_forward(
            info, rows, mixed, own, found[pos], (pos, 0), bias_all, obias_all, 352, 256, ties
        )
        ties = ()
        kept.append((parts, rows, quant, slope, other))
    if not cot_found:
        if layers == 1:
            line.start(one_step(line, pick(cots, 1 - side), cot_found))
            line.tick()
        line.tick()
    out = (stream * live[:, 0:1]).astype(B16)
    grad, line.mark = join_features(info, line.gate(pick(cots, side)), cot_found[0], live)

    block = units // count
    line.start(one_step(line, features(out, 1 - side), out_found), tied=True)

    grads_found = [[] for _ in range(layers)]
    pack_found = [[] for _ in range(layers)]
    gathered = [None] * layers
    chan_grads = ()

    def gather_ready():
        for pos in reversed(range(layers)):
            if gathered[pos] is None and grads_found[pos]:
                gathered[pos] = lax.all_gather(grads_found[pos][0], "dp")

    for pos in reversed(range(layers)):
        parts, rows, quant, slope, other = kept[pos]
        back, small, keep = None, 0.0, []
        for halves in ((0,), (1,)):
            ties = line.tick()
            gather_ready()
            *sums, part_small, back, line.mark = chan_backward(
                info, grad, rows, quant, slope, own, other, pos, back, count // 2, halves, ties
            )
            small = small + part_small
            if 0 in halves:
                steps = upper_grad_steps if pos > 0 else lowest_grad_steps
                above = pack_found[pos + 1] if pos + 1 < layers else []
                line.start(steps(line, sums[0], keep, above, grads_found[pos]))
            if 1 in halves:
                keep.append(sums[-1])
        ties = line.tick()
        gather_ready()
        base, token_grads, smalls = (), [], []
        for k in range(2):
            following, token_grad, token_small, line.mark = token_backward(
                grad,
                back,
                parts[k],
                pos,
                token_params[k],
                counts[k],
                padded[k],
                offsets[k],
                base,
                ties,
            )
            ties = ()
            base = (following,)
            token_grads.append(token_grad)
            smalls.append(token_small)
        grad = following
        pieces = token_grads + smalls + [small]
        size = sum(p.shape[0] for p in pieces)
        fill = jnp.zeros((-size % (8 * count), width), F32)
        pack = jnp.concatenate(pieces + [fill], 0).astype(B16)
        if pos > 0:
            line.start(pack_near_steps(line, pack, pack_found[pos]), first=True)
        else:
            line.start(pack_all_steps(line, pack, pack_found[0]))

    grad_found = []
    line.start(one_step(line, features(grad, 1 - side).astype(B16), grad_found, 3))
    done, ticks = layers, 0
    while line.flows:
        line.tick()
        ticks += 1
        gather_ready()
        also = []
        if done > 1 and ticks > 1:
            done -= 1
            *chan_grads, mark = assemble(
                gathered[done], places, done, layers, block, tuple(chan_grads)
            )
            also = [mark]
        if any(flow["got"] for flow in line.flows):
            line.arrived(*also)
    outs = to_features(features(out, side), line.gate(out_found[0]))
    grads = to_features(features(grad, side), line.gate(grad_found[0].astype(F32)))
    while done:
        done -= 1
        *chan_grads, _ = assemble(gathered[done], places, done, layers, block, tuple(chan_grads))
    pack_rows = pack.shape[0]
    pack = pack_found[0] + [g[:, 2 * block :] for g in gathered[: layers - 1]]
    pack = jnp.stack([p.reshape(pack_rows, width) for p in pack])
    hidden_tok = mix_bias_small.shape[1]
    token_parts = []
    at = 0
    for k in range(2):
        block = pack[:, at : at + patches[k]].astype(F32)
        token_parts.append((block[:, :, :hidden_tok], jnp.swapaxes(block[:, :, hidden_tok:], 1, 2)))
        at += padded[k]
    small = pack[:, at : at + 24].astype(F32)
    mine = lax.dynamic_slice_in_dim(small, side * own_width, own_width, 2)
    norm_g = mine[:, 0:4] + mine[:, 8:12]
    cbias = lax.dynamic_slice_in_dim(small[:, 17:21].reshape(layers, -1), side * units, units, 1)
    return (
        outs[0],
        outs[1],
        grads[0],
        grads[1],
        norm_g[:, 0:2],
        norm_g[:, 2:4],
        token_parts[0][0],
        small[:, 4, :hidden_tok],
        token_parts[0][1],
        small[:, 5, : patches[0]],
        token_parts[1][0],
        small[:, 12, :hidden_tok],
        token_parts[1][1],
        small[:, 13, : patches[1]],
        chan_grads[0],
        cbias,
        chan_grads[1],
        mine[:, 16],
    )


def solution(mesh):
    in_specs = (
        P("dp", None, "mp"),
        P("dp", None, "mp"),
        P("dp", None),
        P(None, None, "mp"),
        P(None, None, "mp"),
        P(),
        P(),
        P(),
        P(),
        P(),
        P(),
        P(),
        P(),
        P(None, None, "mp"),
        P(None, "mp"),
        P(None, "mp", None),
        P(None, "mp"),
        P("dp", None, "mp"),
        P("dp", None, "mp"),
    )
    out_specs = (
        P("dp", None, "mp"),
        P("dp", None, "mp"),
        P("dp", None, "mp"),
        P("dp", None, "mp"),
        P(None, None, "mp"),
        P(None, None, "mp"),
        P(),
        P(),
        P(),
        P(),
        P(),
        P(),
        P(),
        P(),
        P(None, None, "mp"),
        P(None, "mp"),
        P(None, "mp", None),
        P(None, "mp"),
    )
    body = image_body if image_split(mesh) else split_body
    return jax.shard_map(body, mesh=mesh, in_specs=in_specs, out_specs=out_specs, check_vma=False)
```

```python
import functools

import jax
import jax.numpy as jnp
from jax import lax
from jax.experimental import pallas as pl
from jax.experimental.pallas import tpu as pltpu
from jax.sharding import PartitionSpec as P

EPS = 1e-06
F32 = jnp.float32
B16 = jnp.bfloat16


def gelu_exact(field):
    return jax.nn.gelu(field, approximate=False)


def gelu_pull(point, grad_in):
    return jax.vjp(gelu_exact, point)[1](grad_in)[0]


def norm_apply(stream, gain_vec, shift_vec, feature_count):
    totals = lax.psum(
        (
            jnp.sum(stream[0], -1),
            jnp.sum(stream[0] * stream[0], -1),
            jnp.sum(stream[1], -1),
            jnp.sum(stream[1] * stream[1], -1),
        ),
        "mp",
    )
    centred_list, scale_list, normed_list = ([], [], [])
    for set_index in range(2):
        row_mean = totals[2 * set_index] / feature_count
        spread = totals[2 * set_index + 1] / feature_count - row_mean * row_mean
        row_scale = lax.rsqrt(spread + EPS)
        centred = (stream[set_index] - row_mean[..., None]) * row_scale[..., None]
        centred_list.append(centred)
        scale_list.append(row_scale)
        normed_list.append(centred * gain_vec + shift_vec)
    return (centred_list, scale_list, normed_list)


def norm_back(grad_list, centred_list, scale_list, gain_vec, feature_count):
    scaled = [grad_list[0] * gain_vec, grad_list[1] * gain_vec]
    totals = lax.psum(
        (
            jnp.sum(scaled[0], -1),
            jnp.sum(scaled[0] * centred_list[0], -1),
            jnp.sum(scaled[1], -1),
            jnp.sum(scaled[1] * centred_list[1], -1),
        ),
        "mp",
    )
    back_list = []
    for set_index in range(2):
        inner_term = (
            scaled[set_index]
            - totals[2 * set_index][..., None] / feature_count
            - centred_list[set_index] * (totals[2 * set_index + 1][..., None] / feature_count)
        )
        back_list.append(scale_list[set_index][..., None] * inner_term)
    gain_grad = jnp.sum(grad_list[0] * centred_list[0], axis=(0, 1)) + jnp.sum(
        grad_list[1] * centred_list[1], axis=(0, 1)
    )
    shift_grad = jnp.sum(grad_list[0], axis=(0, 1)) + jnp.sum(grad_list[1], axis=(0, 1))
    return (back_list, gain_grad, shift_grad)


def split_body(
    image_small,
    image_large,
    image_counts,
    norm_gain,
    norm_shift,
    mix_in_small,
    mix_bias_small,
    mix_out_small,
    mix_obias_small,
    mix_in_large,
    mix_bias_large,
    mix_out_large,
    mix_obias_large,
    chan_in,
    chan_bias,
    chan_out,
    chan_obias,
    cot_small,
    cot_large,
):
    feature_count = norm_gain.shape[2] * lax.axis_size("mp")
    layers = norm_gain.shape[0]
    slot_count = (image_small.shape[0], image_large.shape[0])
    live_masks = [
        (jnp.arange(slot_count[k], dtype=jnp.int32) < image_counts[0, k]).astype(F32)[:, None, None]
        for k in range(2)
    ]
    mixers = (
        (mix_in_small, mix_bias_small, mix_out_small, mix_obias_small),
        (mix_in_large, mix_bias_large, mix_out_large, mix_obias_large),
    )
    stream = [image_small.astype(F32), image_large.astype(F32)]
    kept_state = []
    for layer_pos in range(layers):
        centred_one, scale_one, normed_one = norm_apply(
            stream, norm_gain[layer_pos, 0], norm_shift[layer_pos, 0], feature_count
        )
        lowered, pre_list, act_list, mixed_list = ([], [], [], [])
        for set_index in range(2):
            token_in, token_bias, token_out, token_obias = mixers[set_index]
            normed_low = normed_one[set_index].astype(B16)
            pre_act = (
                jnp.einsum(
                    "nsc,sh->nhc", normed_low, token_in[layer_pos], preferred_element_type=F32
                )
                + token_bias[layer_pos][None, :, None]
            )
            activated = gelu_exact(pre_act).astype(B16)
            branch = jnp.einsum(
                "nhc,hs->nsc", activated, token_out[layer_pos], preferred_element_type=F32
            )
            mixed_list.append(stream[set_index] + branch + token_obias[layer_pos][None, :, None])
            lowered.append(normed_low)
            pre_list.append(pre_act)
            act_list.append(activated)
        centred_two, scale_two, normed_two = norm_apply(
            mixed_list, norm_gain[layer_pos, 1], norm_shift[layer_pos, 1], feature_count
        )
        normed_rows = (normed_two[0].astype(B16), normed_two[1].astype(B16))
        weight_in = chan_in[layer_pos]
        gathered_rows = None
        hidden = (
            jnp.dot(
                lax.all_gather(normed_rows[0], "mp", axis=2, tiled=True),
                weight_in,
                preferred_element_type=F32,
            ),
            jnp.dot(
                lax.all_gather(normed_rows[1], "mp", axis=2, tiled=True),
                weight_in,
                preferred_element_type=F32,
            ),
        )
        hidden = [hidden[k] + chan_bias[layer_pos] for k in range(2)]
        hidden_low = [gelu_exact(hidden[k]).astype(B16) for k in range(2)]
        partial_value = [
            jnp.dot(hidden_low[k], chan_out[layer_pos], preferred_element_type=F32)
            for k in range(2)
        ]
        summed = (
            lax.psum_scatter(
                partial_value[0].astype(jnp.bfloat16), "mp", scatter_dimension=2, tiled=True
            ).astype(jnp.float32),
            lax.psum_scatter(
                partial_value[1].astype(jnp.bfloat16), "mp", scatter_dimension=2, tiled=True
            ).astype(jnp.float32),
        )
        kept_state.append(
            (
                centred_one,
                scale_one,
                lowered,
                pre_list,
                act_list,
                centred_two,
                scale_two,
                normed_rows,
                gathered_rows,
                hidden,
                hidden_low,
            )
        )
        stream = [mixed_list[k] + summed[k] + chan_obias[layer_pos] for k in range(2)]
    out_list = [(stream[k] * live_masks[k]).astype(B16) for k in range(2)]
    grad_stream = [cot_small.astype(F32) * live_masks[0], cot_large.astype(F32) * live_masks[1]]
    mix_terms = [None] * layers
    chan_terms = [None] * layers
    for layer_pos in reversed(range(layers)):
        (
            centred_one,
            scale_one,
            lowered,
            pre_list,
            act_list,
            centred_two,
            scale_two,
            normed_rows,
            gathered_rows,
            hidden,
            hidden_low,
        ) = kept_state[layer_pos]
        grad_low = (grad_stream[0].astype(B16), grad_stream[1].astype(B16))
        obias_grad = jnp.sum(grad_low[0].astype(F32), axis=(0, 1)) + jnp.sum(
            grad_low[1].astype(F32), axis=(0, 1)
        )
        gathered_grad = (
            lax.all_gather(grad_low[0], "mp", axis=2, tiled=True),
            lax.all_gather(grad_low[1], "mp", axis=2, tiled=True),
        )
        out_grad = jnp.einsum(
            "nsf,nsc->fc", hidden_low[0], gathered_grad[0], preferred_element_type=F32
        ) + jnp.einsum("nsf,nsc->fc", hidden_low[1], gathered_grad[1], preferred_element_type=F32)
        hidden_grad = [
            gelu_pull(
                hidden[k],
                jnp.einsum(
                    "nsc,fc->nsf", gathered_grad[k], chan_out[layer_pos], preferred_element_type=F32
                ),
            ).astype(B16)
            for k in range(2)
        ]
        bias_grad = jnp.sum(hidden_grad[0].astype(F32), axis=(0, 1)) + jnp.sum(
            hidden_grad[1].astype(F32), axis=(0, 1)
        )
        contribution = jnp.einsum(
            "nsk,nsf->kf",
            lax.all_gather(normed_rows[0], "mp", axis=2, tiled=True),
            hidden_grad[0],
            preferred_element_type=F32,
        ) + jnp.einsum(
            "nsk,nsf->kf",
            lax.all_gather(normed_rows[1], "mp", axis=2, tiled=True),
            hidden_grad[1],
            preferred_element_type=F32,
        )
        back_terms = [
            jnp.einsum(
                "nsf,cf->nsc", hidden_grad[k], chan_in[layer_pos], preferred_element_type=F32
            )
            for k in range(2)
        ]
        back_rows = (
            lax.psum_scatter(
                back_terms[0].astype(jnp.bfloat16), "mp", scatter_dimension=2, tiled=True
            ).astype(jnp.float32),
            lax.psum_scatter(
                back_terms[1].astype(jnp.bfloat16), "mp", scatter_dimension=2, tiled=True
            ).astype(jnp.float32),
        )
        norm_grad_two, gain_two, shift_two = norm_back(
            back_rows, centred_two, scale_two, norm_gain[layer_pos, 1], feature_count
        )
        mid_grad = [grad_stream[k] + norm_grad_two[k] for k in range(2)]
        token_terms = []
        norm_input = []
        for set_index in range(2):
            token_in, token_bias, token_out, token_obias = mixers[set_index]
            token_grad = mid_grad[set_index].astype(B16)
            token_obias_grad = jnp.sum(token_grad.astype(F32), axis=(0, 2))
            token_out_grad = jnp.einsum(
                "nhc,nsc->hs", act_list[set_index], token_grad, preferred_element_type=F32
            )
            act_grad = jnp.einsum(
                "nsc,hs->nhc", token_grad, token_out[layer_pos], preferred_element_type=F32
            )
            pre_grad = gelu_pull(pre_list[set_index], act_grad).astype(B16)
            token_bias_grad = jnp.sum(pre_grad.astype(F32), axis=(0, 2))
            token_in_grad = jnp.einsum(
                "nsc,nhc->sh", lowered[set_index], pre_grad, preferred_element_type=F32
            )
            norm_input.append(
                jnp.einsum("nhc,sh->nsc", pre_grad, token_in[layer_pos], preferred_element_type=F32)
            )
            token_terms += [token_in_grad, token_bias_grad, token_out_grad, token_obias_grad]
        norm_grad_one, gain_one, shift_one = norm_back(
            norm_input, centred_one, scale_one, norm_gain[layer_pos, 0], feature_count
        )
        grad_stream = [mid_grad[k] + norm_grad_one[k] for k in range(2)]
        chan_local = (
            contribution,
            bias_grad,
            out_grad,
            obias_grad,
            jnp.stack([gain_one, gain_two]),
            jnp.stack([shift_one, shift_two]),
        )
        mix_terms[layer_pos] = lax.psum(
            (
                token_terms[0],
                token_terms[1],
                token_terms[2],
                token_terms[3],
                token_terms[4],
                token_terms[5],
                token_terms[6],
                token_terms[7],
            ),
            ("dp", "mp"),
        )
        chan_terms[layer_pos] = (
            lax.psum(chan_local[0].astype(jnp.bfloat16), "dp").astype(jnp.float32),
            lax.psum(chan_local[1].astype(jnp.bfloat16), "dp").astype(jnp.float32),
            lax.psum(chan_local[2].astype(jnp.bfloat16), "dp").astype(jnp.float32),
            lax.psum(chan_local[3].astype(jnp.bfloat16), "dp").astype(jnp.float32),
            lax.psum(chan_local[4].astype(jnp.bfloat16), "dp").astype(jnp.float32),
            lax.psum(chan_local[5].astype(jnp.bfloat16), "dp").astype(jnp.float32),
        )
    mix_stacked = [jnp.stack([mix_terms[pos][item] for pos in range(layers)]) for item in range(8)]
    chan_stacked = [
        jnp.stack([chan_terms[pos][item] for pos in range(layers)]) for item in range(6)
    ]
    return (
        out_list[0],
        out_list[1],
        grad_stream[0],
        grad_stream[1],
        chan_stacked[4],
        chan_stacked[5],
        mix_stacked[0],
        mix_stacked[1],
        mix_stacked[2],
        mix_stacked[3],
        mix_stacked[4],
        mix_stacked[5],
        mix_stacked[6],
        mix_stacked[7],
        chan_stacked[0],
        chan_stacked[1],
        chan_stacked[2],
        chan_stacked[3],
    )


LANES = 128
SIDE, CORE, QUARTER, PLACE = range(4)
VMEM_LIMIT = 56 << 20
COST_SCALE = 200


def gelu_pair(point):
    below = 0.5 + 0.5 * lax.erf(point * 0.7071067811865476)
    bell = jnp.exp(point * point * -0.5) * 0.3989422804014327
    return point * below, below + point * bell


def kernel_call(
    kernel, grid, in_specs, out_specs, out_shape, scratch=(), cost=None, aliases=None, prefetch=0
):
    return pl.pallas_call(
        kernel,
        grid_spec=pltpu.PrefetchScalarGridSpec(
            num_scalar_prefetch=prefetch,
            grid=grid,
            in_specs=in_specs,
            out_specs=out_specs,
            scratch_shapes=list(scratch),
        ),
        out_shape=out_shape,
        compiler_params=pltpu.CompilerParams(vmem_limit_bytes=VMEM_LIMIT),
        cost_estimate=cost,
        input_output_aliases=aliases or {},
    )


def cost_of(flops, nbytes):
    return pl.CostEstimate(
        flops=int(COST_SCALE * flops), bytes_accessed=int(COST_SCALE * nbytes), transcendentals=0
    )


def mark_spec():
    return pl.BlockSpec(memory_space=pltpu.SMEM), jax.ShapeDtypeStruct((1, 1), F32)


def column(row, size):
    pad = -row.shape[1] % LANES
    if pad:
        row = jnp.concatenate([row, jnp.zeros((1, pad), F32)], 1)
    return jnp.broadcast_to(row, (8, row.shape[1])).T[:size, 0:1]


def pad_rows(value, size):
    if value.shape[0] == size:
        return value
    return jnp.concatenate([value, jnp.zeros((size - value.shape[0], value.shape[1]), value.dtype)], 0)


def dims_nt(left, right):
    return lax.dot_general(left, right, (((1,), (1,)), ((), ())), preferred_element_type=F32)


def dims_tn(left, right):
    return lax.dot_general(left, right, (((0,), (0,)), ((), ())), preferred_element_type=F32)


def dims_nn(left, right):
    return jnp.dot(left, right, preferred_element_type=F32)


def norm_block(field):
    centred = field - jnp.mean(field, -1, keepdims=True)
    scale = lax.rsqrt(jnp.mean(centred * centred, -1, keepdims=True) + EPS)
    return centred * scale, scale


def token_forward_kernel(x_ref, norm_ref, in_ref, bias_ref, out_ref, obias_ref, *rest):
    (
        mixed_ref,
        rows_ref,
        low_ref,
        act_ref,
        slope_ref,
        vhat_one_ref,
        vhat_two_ref,
        scale_ref,
        mark_ref,
    ) = rest[-9:]
    x = x_ref[...]
    size = x.shape[0]
    vhat, scale = norm_block(x)
    vhat_one_ref[...] = vhat.astype(B16)
    low = (vhat * norm_ref[0:1, :] + norm_ref[2:3, :]).astype(B16)
    low_ref[...] = low
    point = dims_tn(pad_rows(in_ref[...], size), low) + column(bias_ref[...], act_ref.shape[0])
    act, slope = gelu_pair(point)
    act = act.astype(B16)
    act_ref[...] = act
    slope_ref[...] = slope.astype(B16)
    mixed = x + dims_nn(pad_rows(out_ref[...], size), act) + column(obias_ref[...], size)
    mixed_ref[...] = mixed
    vhat, scale_two = norm_block(mixed)
    vhat_two_ref[...] = vhat.astype(B16)
    rows_ref[...] = (vhat * norm_ref[1:2, :] + norm_ref[3:4, :]).astype(B16)
    scale_ref[:, 0:1] = scale
    scale_ref[:, 1:2] = scale_two
    mark_ref[0, 0] = 0.0


def row_block(patches, width, offset):
    return pl.BlockSpec(
        (pl.Element(patches), pl.Element(width)),
        lambda i: ((offset // 16 + i * (patches // 16)) * 16, 0),
    )


def whole_spec(array):
    return pl.BlockSpec(array.shape, lambda *i: (0, 0))


def free_specs(arrays):
    return [pl.BlockSpec(memory_space=pl.ANY)] * len(arrays)


def layer_spec(array, pos):
    return pl.BlockSpec(
        (None,) + array.shape[1:], lambda *i: (pos,) + (0,) * (array.ndim - 1)
    )


def token_forward(x, pos, params, images, patches, offset, base, after=()):
    total, width = x.shape
    hidden = params[1].shape[2]
    rows = images * patches
    block = lambda size, lanes: pl.BlockSpec((size, lanes), lambda i: (i, 0))
    placed = row_block(patches, width, offset)
    shape = jax.ShapeDtypeStruct
    mark = mark_spec()
    return kernel_call(
        token_forward_kernel,
        (images,),
        [placed] + [layer_spec(a, pos) for a in params] + free_specs(base + after),
        [placed, placed]
        + [block(patches, width)]
        + [block(hidden, width)] * 2
        + [block(patches, width)] * 2
        + [block(patches, LANES), mark[0]],
        [
            shape((total, width), F32),
            shape((total, width), B16),
            shape((rows, width), B16),
            shape((images * hidden, width), B16),
            shape((images * hidden, width), B16),
            shape((rows, width), B16),
            shape((rows, width), B16),
            shape((rows, LANES), F32),
            mark[1],
        ],
        aliases={6 + i: i for i in range(len(base))},
        cost=cost_of(4 * rows * hidden * width, 30 * rows * width),
    )(x, *params, *base, *after)


def join_kernel(info_ref, own_ref, got_ref, live_ref, joined_ref, mark_ref):
    own, got = own_ref[...].astype(F32), got_ref[...].astype(F32)
    first = info_ref[SIDE] == 0
    live = live_ref[:, 0:1]
    half = own.shape[1]
    joined_ref[:, :half] = jnp.where(first, own, got) * live
    joined_ref[:, half:] = jnp.where(first, got, own) * live
    mark_ref[0, 0] = 0.0


def join_features(info, own, got, live, tiles=4):
    rows, half = own.shape
    block = lambda lanes: pl.BlockSpec((rows // tiles, lanes), lambda i, _: (i, 0))
    mark = mark_spec()
    return kernel_call(
        join_kernel,
        (tiles,),
        [block(half), block(half), block(LANES)],
        [block(2 * half), mark[0]],
        [jax.ShapeDtypeStruct((rows, 2 * half), F32), mark[1]],
        prefetch=1,
        cost=cost_of(0, 12 * rows * half),
    )(info, own, got, live)


def chan_forward_kernel(
    part,
    info_ref,
    rows_ref,
    mixed_ref,
    in_own_ref,
    out_own_ref,
    in_near_ref,
    in_far_ref,
    out_near_ref,
    out_far_ref,
    bias_ref,
    obias_ref,
    *rest,
):
    quant_ref, slope_ref, total_ref, in_other_ref, out_other_ref, mark_ref = rest[-6:]
    mark_ref[0, 0] = 0.0

    @pl.when(pl.program_id(0) == 0)
    def _():
        place = info_ref[QUARTER]
        for pieces, other_ref in (
            ((in_near_ref, in_far_ref), in_other_ref),
            ((out_near_ref, out_far_ref), out_other_ref),
        ):
            size = pieces[0].shape[1]
            for k in range(4):
                at = pl.multiple_of((place ^ k) * size, size)
                other_ref[pl.ds(at, size), :] = pieces[k // 2][k % 2]

    rows = rows_ref[...]
    total = mixed_ref[...] + obias_ref[...]
    units = in_own_ref.shape[1]
    for side, (in_ref, out_ref) in enumerate(
        ((in_own_ref, out_own_ref), (in_other_ref, out_other_ref))
    ):
        for at in range(0, units, part):
            lanes = slice(at, at + part)
            place = slice(side * units + at, side * units + at + part)
            point = dims_nn(rows, in_ref[:, lanes]) + bias_ref[:, place]
            quant, slope = gelu_pair(point)
            quant = quant.astype(B16)
            quant_ref[:, place] = quant
            slope_ref[:, place] = slope.astype(B16)
            total = total + dims_nn(quant, out_ref[lanes, :])
    total_ref[...] = total


def chan_forward(info, rows, mixed, own, found, layer, bias, obias, tile, part, after=()):
    pos, at = layer
    count, width = rows.shape
    units = bias.shape[2]
    half = units // 2
    mark = mark_spec()
    tiled = pl.BlockSpec((tile, width), lambda i, _: (i, 0))
    lanes = pl.BlockSpec((tile, units), lambda i, _: (i, 0))
    once = lambda rows, cols: pl.BlockSpec((rows, cols), lambda i, _: (0, 0))
    layered = lambda a: pl.BlockSpec((None,) + a.shape[1:], lambda i, _: (pos, 0, 0))
    pieces = lambda a: pl.BlockSpec(
        (a.shape[0], None) + a.shape[2:], lambda i, _: (0, at, 0, 0)
    )
    return kernel_call(
        functools.partial(chan_forward_kernel, part),
        (count // tile,),
        [tiled, tiled]
        + [layered(a) for a in own]
        + [pieces(a) for a in found]
        + [layered(bias), layered(obias)]
        + free_specs(after),
        [lanes, lanes, tiled, once(width, half), once(half, width), mark[0]],
        [
            jax.ShapeDtypeStruct((count, units), B16),
            jax.ShapeDtypeStruct((count, units), B16),
            jax.ShapeDtypeStruct((count, width), F32),
            jax.ShapeDtypeStruct((width, half), B16),
            jax.ShapeDtypeStruct((half, width), B16),
            mark[1],
        ],
        prefetch=1,
        cost=cost_of(4 * count * units * width, 4 * count * units + 10 * count * width),
    )(info, rows, mixed, *own, *found, bias, obias, *after)


def chan_backward_kernel(
    blocks,
    halves,
    info_ref,
    grad_ref,
    rows_ref,
    quant_ref,
    slope_ref,
    in_own_ref,
    out_own_ref,
    in_other_ref,
    out_other_ref,
    *rest,
):
    *sum_refs, small_ref, back_ref, mark_ref, low_ref = rest[-4 - len(halves) :]
    mark_ref[0, 0] = 0.0
    step = pl.program_id(0)

    @pl.when(step == 0)
    def _():
        low = grad_ref[...].astype(B16)
        low_ref[...] = low
        small_ref[...] = jnp.zeros_like(small_ref)
        if halves[0] == 0:
            small_ref[0:1, :] = jnp.sum(low.astype(F32), 0, keepdims=True)
            back_ref[...] = jnp.zeros_like(back_ref)
        else:
            back_ref[...] = rest[0][...]

    def body(other, keep, in_ref, out_ref, sum_ref):
        low = low_ref[...]
        hidden = (dims_nt(low, out_ref[...]) * slope_ref[...].astype(F32)).astype(B16)
        core = info_ref[CORE] if keep else 1 - info_ref[CORE]
        row = 1 + 2 * (info_ref[SIDE] ^ other) + core
        small_ref[pl.ds(row, 1), :] = jnp.sum(hidden.astype(F32), 0, keepdims=True)
        for item, grads in enumerate(
            (dims_tn(hidden, rows_ref[...]), dims_tn(quant_ref[...], low))
        ):
            size = grads.shape[0] // blocks
            for k in range(blocks):
                part = grads[k * size : (k + 1) * size, :].astype(B16)
                sum_ref[item, k ^ info_ref[PLACE]] = part
        back_ref[...] += dims_nt(hidden, in_ref[...])

    sides = ((in_own_ref, out_own_ref), (in_other_ref, out_other_ref))
    for k in range(2 * len(halves)):
        other, place = 1 - k % 2, k // 2

        @pl.when(step == k)
        def _(other=other, place=place):
            body(other, halves[place], *sides[other], sum_refs[place])


def chan_backward(
    info, grad, rows, quant, slope, own, other, pos, back, blocks, halves, after=()
):
    count, width = rows.shape
    chunk = own[0].shape[2] // 2
    if len(halves) == 2:
        core = lambda s, info: jnp.where(s < 2, 1 - info[CORE], info[CORE])
        which = lambda s: (jnp.minimum(s, 1), jnp.maximum(s - 2, 0))
    else:
        core = lambda s, info: info[CORE] if halves[0] else 1 - info[CORE]
        which = lambda s: (s,)
    lanes = pl.BlockSpec(
        (count, chunk), lambda s, info: (0, 2 * (1 - lax.rem(s, 2)) + core(s, info))
    )
    once = lambda rows, cols: pl.BlockSpec((rows, cols), lambda s, _: (0, 0))
    part = (None, 2, blocks, chunk // blocks, width)
    sums = [
        pl.BlockSpec(part, lambda s, _, i=i: (which(s)[i], 0, 0, 0, 0))
        for i in range(len(halves))
    ]
    extra = () if halves[0] == 0 else (back,)
    mark = mark_spec()
    return kernel_call(
        functools.partial(chan_backward_kernel, blocks, halves),
        (2 * len(halves),),
        [once(count, width), once(count, width), lanes, lanes]
        + [
            pl.BlockSpec((None, width, chunk), lambda s, info: (pos, 0, core(s, info))),
            pl.BlockSpec((None, chunk, width), lambda s, info: (pos, core(s, info), 0)),
            pl.BlockSpec((width, chunk), lambda s, info: (0, core(s, info))),
            pl.BlockSpec((chunk, width), lambda s, info: (core(s, info), 0)),
        ]
        + [once(count, width)] * len(extra)
        + free_specs(after),
        sums + [once(8, width), once(count, width), mark[0]],
        [jax.ShapeDtypeStruct((2,) + part[1:], B16)] * len(halves)
        + [
            jax.ShapeDtypeStruct((8, width), F32),
            jax.ShapeDtypeStruct((count, width), F32),
            mark[1],
        ],
        scratch=[pltpu.VMEM((count, width), B16)],
        prefetch=1,
        cost=cost_of(
            16 * len(halves) * count * chunk * width, 8 * count * chunk + 16 * count * width
        ),
    )(info, grad, rows, quant, slope, *own, *other, *extra, *after)


def assemble_kernel(places, size, all_ref, *rest):
    in_ref, out_ref, mark_ref, scratch = rest[-4:]
    mark_ref[0, 0] = 0.0

    def body(core):
        for i, (in_place, out_place) in enumerate(places):
            if i % 2 == core:
                at = slice(in_place * size, (in_place + 1) * size)
                scratch[at, :] = all_ref[i, 0:size, :].astype(F32)
                at = slice(out_place * size, (out_place + 1) * size)
                out_ref[at, :] = all_ref[i, size : 2 * size, :].astype(F32)
        in_ref[...] = scratch[...].T

    pl.when(pl.program_id(0) == 0)(lambda: body(0))
    pl.when(pl.program_id(0) == 1)(lambda: body(1))


def assemble(gathered, places, pos, layers, size, base):
    count, _, width = gathered.shape
    chunk = count // 2 * size
    mark = mark_spec()
    return kernel_call(
        functools.partial(assemble_kernel, places, size),
        (2,),
        [pl.BlockSpec(gathered.shape, lambda s: (0, 0, 0))] + free_specs(base),
        [
            pl.BlockSpec((None, width, chunk), lambda s: (pos, 0, s)),
            pl.BlockSpec((None, chunk, width), lambda s: (pos, s, 0)),
            mark[0],
        ],
        [
            jax.ShapeDtypeStruct((layers, width, 2 * chunk), F32),
            jax.ShapeDtypeStruct((layers, 2 * chunk, width), F32),
            mark[1],
        ],
        scratch=[pltpu.VMEM((chunk, width), F32)],
        aliases={1 + i: i for i in range(len(base))},
        cost=cost_of(0, 24 * chunk * width),
    )(gathered, *base)


def mark_kernel(*refs):
    refs[-1][0, 0] = 0.0


def mark_after(*arrays):
    mark = mark_spec()
    return kernel_call(mark_kernel, (1,), free_specs(arrays), mark[0], mark[1])(*arrays)


def norm_block_back(grad, vhat, scale, gain):
    scaled = grad * gain
    inner = (
        scaled
        - jnp.mean(scaled, -1, keepdims=True)
        - vhat * jnp.mean(scaled * vhat, -1, keepdims=True)
    )
    return scale * inner, jnp.sum(grad * vhat, 0, keepdims=True), jnp.sum(grad, 0, keepdims=True)


def token_backward_kernel(
    grad_ref,
    back_ref,
    vhat_two_ref,
    scale_ref,
    act_ref,
    slope_ref,
    low_ref,
    vhat_one_ref,
    norm_ref,
    in_ref,
    out_ref,
    *rest,
):
    next_ref, grads_ref, small_ref, mark_ref = rest[-4:]
    mark_ref[0, 0] = 0.0
    first = pl.program_id(0) == 0

    def add(ref, where, value):
        @pl.when(first)
        def _():
            ref[where] = value

        @pl.when(jnp.logical_not(first))
        def _():
            ref[where] += value

    patches, width = low_ref.shape
    hidden = act_ref.shape[0]
    ones = jnp.ones((8, width), B16)
    pl.when(first)(lambda: small_ref.__setitem__((Ellipsis,), jnp.zeros_like(small_ref)))
    dv, gain_two, shift_two = norm_block_back(
        back_ref[...], vhat_two_ref[...].astype(F32), scale_ref[:, 1:2], norm_ref[1:2, :]
    )
    mid = grad_ref[...].astype(F32) + dv
    low = mid.astype(B16)
    small_ref[5:6, :patches] += dims_nt(ones, low)[0:1, :]
    add(grads_ref, (slice(None), slice(hidden, None)), dims_nt(low, act_ref[...]))
    point = (dims_tn(pad_rows(out_ref[...], patches), low) * slope_ref[...].astype(F32)).astype(B16)
    small_ref[4:5, :hidden] += dims_nt(ones, point)[0:1, :]
    add(grads_ref, (slice(None), slice(0, hidden)), dims_nt(low_ref[...], point))
    dv, gain_one, shift_one = norm_block_back(
        dims_nn(pad_rows(in_ref[...], patches), point),
        vhat_one_ref[...].astype(F32),
        scale_ref[:, 0:1],
        norm_ref[0:1, :],
    )
    next_ref[...] = mid + dv
    for i, value in enumerate((gain_one, gain_two, shift_one, shift_two)):
        small_ref[i : i + 1, :] += value


def token_backward(grad, back, kept, pos, params, images, patches, offset, base, after=()):
    low, act, slope, vhat_one, vhat_two, scale = kept
    norm, w_in, _, w_out, _ = params
    total, width = grad.shape
    hidden = w_in.shape[2]
    rows = images * patches
    block = lambda size, lanes: pl.BlockSpec((size, lanes), lambda i: (i, 0))
    placed = row_block(patches, width, offset)
    shape = lambda r, c: jax.ShapeDtypeStruct((r, c), F32)
    outs = [shape(patches, 2 * hidden), shape(8, width)]
    mark = mark_spec()
    return kernel_call(
        token_backward_kernel,
        (images,),
        [placed, placed, block(patches, width), block(patches, LANES)]
        + [block(hidden, width)] * 2
        + [block(patches, width)] * 2
        + [layer_spec(a, pos) for a in (norm, w_in, w_out)]
        + free_specs(base + after),
        [placed] + [whole_spec(a) for a in outs] + [mark[0]],
        [shape(total, width)] + outs + [mark[1]],
        aliases={11 + i: i for i in range(len(base))},
        cost=cost_of(8 * rows * hidden * width, 30 * rows * width),
    )(grad, back, vhat_two, scale, act, slope, low, vhat_one, norm, w_in, w_out, *base, *after)


def image_split(mesh):
    dp = mesh.shape["dp"]
    return mesh.shape["mp"] == 2 and dp >= 8 and dp & (dp - 1) == 0


def exchange(value, mask, over_mp):
    count = lax.axis_size("dp")
    if not mask:
        return lax.ppermute(value, "mp", [(0, 1), (1, 0)])
    if not over_mp:
        return lax.ppermute(value, "dp", [(i, i ^ mask) for i in range(count)])
    return lax.ppermute(
        value, ("dp", "mp"), [(i, i ^ (2 * mask + 1)) for i in range(2 * count)]
    )


def dp_bit(bit):
    return (lax.axis_index("dp") >> bit) & 1


def join(value, other, flag, axis=0):
    return jnp.where(
        flag == 0,
        jnp.concatenate([value, other], axis),
        jnp.concatenate([other, value], axis),
    )


class Transfers:
    def __init__(self):
        self.flows = []
        self.mark = None

    def start(self, steps, first=False, tied=False):
        flow = {"steps": steps, "got": None, "tied": tied}
        self.flows.insert(0 if first else len(self.flows), flow)
        return flow

    def step(self, flow):
        try:
            if flow["got"] is None:
                sends = next(flow["steps"])
            else:
                sends = flow["steps"].send(flow["got"])
        except StopIteration:
            self.flows.remove(flow)
            return list(flow["got"]) if flow["tied"] else []
        flow["got"] = [exchange(value, *masks) for value, *masks in sends]
        return [send[0] for send in sends]

    def tick(self):
        ties = []
        for flow in list(self.flows):
            ties += self.step(flow)
        return tuple(ties)

    def finish(self, flow):
        self.step(flow)

    def arrived(self, *also):
        self.mark = mark_after(*[got for flow in self.flows for got in flow["got"]], *also)

    def zero(self):
        return self.mark[0, 0]

    def gate(self, value):
        return value if self.mark is None else value + self.zero().astype(value.dtype)

    def add(self, *values):
        total = values[0].astype(F32)
        for value in values[1:]:
            total = total + value.astype(F32)
        return (total + self.zero()).astype(B16)


def one_step(line, value, found, delay=0):
    for _ in range(delay):
        yield []
    (got,) = yield [(line.gate(value), 0, 1)]
    found.append(got)


def fetch_steps(line, weights, pos, found):
    part = dp_bit(0) * 2 + dp_bit(1)
    sends = []
    for weight in weights:
        size = weight.shape[1] // 4
        quarter = lax.dynamic_slice(weight, (pos, part * size, 0), (1, size, weight.shape[2]))
        sends.append(line.gate(quarter))
    near = yield [(s, 0, 1) for s in sends]
    got = yield [(line.gate(s), 2, 0) for s in near]
    pairs = [line.gate(jnp.stack(p)) for p in zip(near, got)]
    far = yield [(s, 1, 0) for s in pairs]
    found += [pairs[0], far[0], pairs[1], far[1]]


def far_blocks(line, value):
    sends = [(value[k], k << 2, 0) for k in range(1, len(value))]
    return value[0], sends


def plain_sum(*values):
    total = values[0].astype(F32)
    for value in values[1:]:
        total = total + value.astype(F32)
    return total.astype(B16)


def upper_grad_steps(line, send, keep, pack, found):
    (got,) = yield [(send, 1, 0)]
    keep = keep[0]
    half = keep.shape[2] // 2
    low, high = slice(half), slice(half, None)
    sum_of = lambda side, blocks: line.add(keep[side, :, blocks], got[side, :, blocks])
    own = [sum_of(1, low), sum_of(1, high)]
    other = [sum_of(0, low), sum_of(0, high)]
    (got,) = yield [(other[1], 0, 1)]
    own[1] = line.add(own[1], got)
    got = yield [(other[0], 0, 1), (own[1], 2, 0)]
    own = line.add(own[0], *got)
    own = jnp.concatenate([own[0], own[1], *pack], 1)
    mine, sends = far_blocks(line, own)
    got = yield sends
    found.append(plain_sum(mine, *got))


def lowest_grad_steps(line, send, keep, pack, found):
    (got,) = yield [(send, 1, 0)]
    keep = keep[0]
    half = keep.shape[2] // 2
    low, high, every = slice(half), slice(half, None), slice(None)
    sum_of = lambda side, item, blocks: line.add(keep[side, item, blocks], got[side, item, blocks])
    in_other, in_low, in_high = sum_of(0, 0, every), sum_of(1, 0, low), sum_of(1, 0, high)
    out_away = sum_of(every, 1, high)
    out_own, out_other = sum_of(1, 1, low), sum_of(0, 1, low)
    got = yield [(in_other, 0, 1), (out_away, 2, 0)]
    in_low, in_high = line.add(in_low, got[0][:half]), line.add(in_high, got[0][half:])
    out_other, out_own = line.add(out_other, got[1][0]), line.add(out_own, got[1][1])
    got = yield [(in_high, 2, 0), (out_other, 0, 1)]
    own = jnp.concatenate([line.add(in_low, got[0]), line.add(out_own, got[1]), *pack], 1)
    mine, sends = far_blocks(line, own)
    got = yield sends
    found.append(line.add(mine, *got))


def pack_near_steps(line, pack, found):
    count = lax.axis_size("dp")
    here = lax.axis_index("dp")
    pack = pack.reshape(count // 4, 2, 2, -1, pack.shape[1])
    near = lambda value, bit, k, axis: lax.dynamic_index_in_dim(value, dp_bit(bit) ^ k, axis, False)
    (got,) = yield [(line.gate(near(pack, 0, 1, 2)), 1, 0)]
    pack = line.add(near(pack, 0, 0, 2), got)
    (got,) = yield [(near(pack, 1, 1, 1), 2, 0)]
    mine = line.add(near(pack, 1, 0, 1), got)
    (got,) = yield [(mine, 0, 1)]
    mine = line.add(mine, got)
    far = lambda k: lax.dynamic_index_in_dim(mine, (here >> 2) ^ k, 0, False)
    found.append(jnp.stack([far(k) for k in range(count // 4)]))


def pack_all_steps(line, pack, found):
    near = []
    yield from pack_near_steps(line, pack, near)
    mine, sends = far_blocks(line, near[0])
    got = yield sends
    mine = line.add(mine, *got)
    got = yield [(mine, k << 2, 0) for k in range(1, lax.axis_size("dp") // 4)]
    parts = line.gate(jnp.stack([mine, *got]))
    (got,) = yield [(parts, 2, 0)]
    parts = line.gate(jnp.stack([parts, got], 1))
    (got,) = yield [(parts, 1, 0)]
    parts = jnp.stack([parts, got], 2)
    parts = parts.reshape((-1,) + parts.shape[3:])
    here = lax.axis_index("dp")
    whole = [lax.dynamic_index_in_dim(parts, here ^ k, 0) for k in range(parts.shape[0])]
    found.append(jnp.concatenate(whole))


def block_place(index, bits):
    low = index >> 1
    return (low & 1) << (bits - 2) | low >> 1


def image_body(
    image_small,
    image_large,
    image_counts,
    norm_gain,
    norm_shift,
    mix_in_small,
    mix_bias_small,
    mix_out_small,
    mix_obias_small,
    mix_in_large,
    mix_bias_large,
    mix_out_large,
    mix_obias_large,
    chan_in,
    chan_bias,
    chan_out,
    chan_obias,
    cot_small,
    cot_large,
):
    layers = norm_gain.shape[0]
    own_width = norm_gain.shape[2]
    width = 2 * own_width
    units = chan_bias.shape[1]
    side = lax.axis_index("mp")
    counts = (image_small.shape[0] // 2, image_large.shape[0] // 2)
    patches = (image_small.shape[1], image_large.shape[1])
    padded = tuple(-(-p // 16) * 16 for p in patches)
    offsets = (0, counts[0] * padded[0])

    def pad_patches(field, k, axis):
        widths = [(0, 0)] * field.ndim
        widths[axis] = (0, padded[k] - patches[k])
        return jnp.pad(field, widths)

    def pick(fields, flag):
        parts = []
        for k in range(2):
            part = lax.dynamic_slice_in_dim(fields[k], flag * counts[k], counts[k], 0)
            parts.append(pad_patches(part, k, 1).reshape(-1, own_width))
        return jnp.concatenate(parts, 0)

    def to_features(own, got):
        outs = []
        for k in range(2):
            pair = []
            for v in (own, got):
                v = v[offsets[k] : offsets[k] + counts[k] * padded[k]]
                pair.append(v.reshape(counts[k], padded[k], own_width)[:, : patches[k]])
            outs.append(join(pair[0], pair[1], side, 0))
        return outs

    def features(rows, flag):
        return lax.dynamic_slice_in_dim(rows, flag * own_width, own_width, 1)

    count = lax.axis_size("dp")
    bits = count.bit_length() - 1
    place = block_place(lax.axis_index("dp"), bits)
    info = jnp.stack([side, dp_bit(0), dp_bit(0) * 2 + dp_bit(1), place]).astype(jnp.int32)
    places = [(block_place(i, bits),) * 2 for i in range(count)]

    line = Transfers()
    vectors = jnp.concatenate(
        [norm_gain.reshape(layers, -1), norm_shift.reshape(layers, -1), chan_obias, chan_bias], 1
    )
    live = []
    for k in range(2):
        slot = side * counts[k] + jnp.arange(counts[k], dtype=jnp.int32)
        alive = (slot < image_counts[0, k]).astype(F32)
        live.append(jnp.repeat(alive, padded[k]))
    live = jnp.broadcast_to(jnp.concatenate(live)[:, None], (sum(c * p for c, p in zip(counts, padded)), LANES))
    own = (chan_in, chan_out)
    images = (image_small, image_large)
    cots = (cot_small, cot_large)
    vectors_found, images_found, cot_found, out_found = [], [], [], []
    found = [[] for _ in range(layers)]
    fetches = {0: line.start(fetch_steps(line, own, 0, found[0]))}
    line.tick()
    line.arrived()
    images_flow = line.start(one_step(line, pick(images, 1 - side), images_found))
    vectors_flow = line.start(one_step(line, vectors, vectors_found))
    line.tick()
    line.finish(images_flow)
    line.finish(vectors_flow)
    other_vectors = vectors_found[0]
    line.mark = mark_after(images_found[0])
    if layers > 1:
        fetches[1] = line.start(fetch_steps(line, own, 1, found[1]))
    ties = line.tick()
    stream, line.mark = join_features(
        info, pick(images, side), images_found[0], jnp.ones_like(live)
    )

    mine, theirs = (v[:, : 5 * own_width].reshape(layers, 5, own_width) for v in (vectors, other_vectors))
    whole = join(mine, theirs, side, 2)
    norms, obias_all = whole[:, :4], whole[:, 4:]
    bias_all = jnp.concatenate([chan_bias, other_vectors[:, 5 * own_width :]], 1)[:, None]
    line_of = lambda b: b[:, None, :]
    token_params = (
        (
            norms,
            mix_in_small,
            line_of(mix_bias_small),
            jnp.swapaxes(mix_out_small, 1, 2),
            line_of(mix_obias_small),
        ),
        (
            norms,
            mix_in_large,
            line_of(mix_bias_large),
            jnp.swapaxes(mix_out_large, 1, 2),
            line_of(mix_obias_large),
        ),
    )

    kept = []
    for pos in range(layers):
        if pos > 0:
            if pos == 1:
                line.start(one_step(line, pick(cots, 1 - side), cot_found))
            ties = line.tick()
        parts, base = [], ()
        for k in range(2):
            mixed, rows, *rest, line.mark = token_forward(
                stream, pos, token_params[k], counts[k], padded[k], offsets[k], base, ties
            )
            ties = ()
            base = (mixed, rows)
            parts.append(rest)
        line.finish(fetches[pos])
        if pos + 2 < layers:
            fetches[pos + 2] = line.start(fetch_steps(line, own, pos + 2, found[pos + 2]))
            ties = line.tick()
        quant, slope, stream, *other, line.mark = chan_forward(
            info, rows, mixed, own, found[pos], (pos, 0), bias_all, obias_all, 352, 256, ties
        )
        ties = ()
        kept.append((parts, rows, quant, slope, other))
    if not cot_found:
        if layers == 1:
            line.start(one_step(line, pick(cots, 1 - side), cot_found))
            line.tick()
        line.tick()
    out = (stream * live[:, 0:1]).astype(B16)
    grad, line.mark = join_features(info, line.gate(pick(cots, side)), cot_found[0], live)

    block = units // count
    line.start(one_step(line, features(out, 1 - side), out_found), tied=True)

    grads_found = [[] for _ in range(layers)]
    pack_found = [[] for _ in range(layers)]
    gathered = [None] * layers
    chan_grads = ()

    def gather_ready():
        for pos in reversed(range(layers)):
            if gathered[pos] is None and grads_found[pos]:
                gathered[pos] = lax.all_gather(grads_found[pos][0], "dp")

    for pos in reversed(range(layers)):
        parts, rows, quant, slope, other = kept[pos]
        back, small, keep = None, 0.0, []
        for halves in ((0,), (1,)):
            ties = line.tick()
            gather_ready()
            *sums, part_small, back, line.mark = chan_backward(
                info, grad, rows, quant, slope, own, other, pos, back, count // 2, halves, ties
            )
            small = small + part_small
            if 0 in halves:
                steps = upper_grad_steps if pos > 0 else lowest_grad_steps
                above = pack_found[pos + 1] if pos + 1 < layers else []
                line.start(steps(line, sums[0], keep, above, grads_found[pos]))
            if 1 in halves:
                keep.append(sums[-1])
        ties = line.tick()
        gather_ready()
        base, token_grads, smalls = (), [], []
        for k in range(2):
            following, token_grad, token_small, line.mark = token_backward(
                grad,
                back,
                parts[k],
                pos,
                token_params[k],
                counts[k],
                padded[k],
                offsets[k],
                base,
                ties,
            )
            ties = ()
            base = (following,)
            token_grads.append(token_grad)
            smalls.append(token_small)
        grad = following
        pieces = token_grads + smalls + [small]
        size = sum(p.shape[0] for p in pieces)
        fill = jnp.zeros((-size % (8 * count), width), F32)
        pack = jnp.concatenate(pieces + [fill], 0).astype(B16)
        if pos > 0:
            line.start(pack_near_steps(line, pack, pack_found[pos]), first=True)
        else:
            line.start(pack_all_steps(line, pack, pack_found[0]))

    grad_found = []
    line.start(one_step(line, features(grad, 1 - side).astype(B16), grad_found, 3))
    done, ticks = layers, 0
    while line.flows:
        line.tick()
        ticks += 1
        gather_ready()
        also = []
        if done > 1 and ticks > 1:
            done -= 1
            *chan_grads, mark = assemble(
                gathered[done], places, done, layers, block, tuple(chan_grads)
            )
            also = [mark]
        if any(flow["got"] for flow in line.flows):
            line.arrived(*also)
    outs = to_features(features(out, side), out_found[0])
    grads = to_features(features(grad, side), grad_found[0].astype(F32))
    while done:
        done -= 1
        *chan_grads, _ = assemble(gathered[done], places, done, layers, block, tuple(chan_grads))
    pack_rows = pack.shape[0]
    pack = pack_found[0] + [g[:, 2 * block :] for g in gathered[: layers - 1]]
    pack = jnp.stack([p.reshape(pack_rows, width) for p in pack])
    hidden_tok = mix_bias_small.shape[1]
    token_parts = []
    at = 0
    for k in range(2):
        block = pack[:, at : at + patches[k]].astype(F32)
        token_parts.append((block[:, :, :hidden_tok], jnp.swapaxes(block[:, :, hidden_tok:], 1, 2)))
        at += padded[k]
    small = pack[:, at : at + 24].astype(F32)
    mine = lax.dynamic_slice_in_dim(small, side * own_width, own_width, 2)
    norm_g = mine[:, 0:4] + mine[:, 8:12]
    cbias = lax.dynamic_slice_in_dim(small[:, 17:21].reshape(layers, -1), side * units, units, 1)
    return (
        outs[0],
        outs[1],
        grads[0],
        grads[1],
        norm_g[:, 0:2],
        norm_g[:, 2:4],
        token_parts[0][0],
        small[:, 4, :hidden_tok],
        token_parts[0][1],
        small[:, 5, : patches[0]],
        token_parts[1][0],
        small[:, 12, :hidden_tok],
        token_parts[1][1],
        small[:, 13, : patches[1]],
        chan_grads[0],
        cbias,
        chan_grads[1],
        mine[:, 16],
    )


def solution(mesh):
    in_specs = (
        P("dp", None, "mp"),
        P("dp", None, "mp"),
        P("dp", None),
        P(None, None, "mp"),
        P(None, None, "mp"),
        P(),
        P(),
        P(),
        P(),
        P(),
        P(),
        P(),
        P(),
        P(None, None, "mp"),
        P(None, "mp"),
        P(None, "mp", None),
        P(None, "mp"),
        P("dp", None, "mp"),
        P("dp", None, "mp"),
    )
    out_specs = (
        P("dp", None, "mp"),
        P("dp", None, "mp"),
        P("dp", None, "mp"),
        P("dp", None, "mp"),
        P(None, None, "mp"),
        P(None, None, "mp"),
        P(),
        P(),
        P(),
        P(),
        P(),
        P(),
        P(),
        P(),
        P(None, None, "mp"),
        P(None, "mp"),
        P(None, "mp", None),
        P(None, "mp"),
    )
    body = image_body if image_split(mesh) else split_body
    return jax.shard_map(body, mesh=mesh, in_specs=in_specs, out_specs=out_specs, check_vma=False)
```
